256 devices in a mesh: dp: 32 (over x, z), mp: 8 (over y, core).
Axes of the slice: x: 4, y: 4, z: 8, core: 2. Of those that a mesh axis runs over, the one named last changes fastest.
Arguments:
- tokens: bfloat16 [8192, 4096], P('dp'), may hold values from -6 to 6
- targets: bfloat16 [8192, 4096], P('dp'), may hold values from -6 to 6
- gate_weight: bfloat16 [4096, 5120], P('dp', 'mp'), may hold values from -0.09375 to 0.09375
- up_weight: bfloat16 [4096, 5120], P('dp', 'mp'), may hold values from -0.09375 to 0.09375
- down_weight: bfloat16 [4096, 5120], P('dp', 'mp'), may hold values from -0.078125 to 0.078125
- krylov: float32 [4, 4096, 5120], P(None, 'dp', 'mp'), may hold values from -18 to 18
Outputs:
- next_vector: float32 [4096, 5120], P('dp', 'mp')
- coefficients: float32 [5], replicated
The draws below stay inside these ranges and needn't reach their ends.
All inputs are finite; a program needn't handle non-finite values.
Results may differ from the reference program's by a relative error of at most 0.029.
Values may be sent and summed in bfloat16 or wider, within the bound.
No kernel may reach another device: no remote copies, remote signals or barrier semaphores. Data moves between devices by JAX's collectives and lax.ppermute only.
A program may use at most 128 MiB of HBM per device.

```python
import math
import jax
import jax.numpy as jnp
from jax import lax

D = 4096
FF = 5120
TOK_DEV = 256
KRYLOV = 4
TOKENS = 8192
N_DP = 32
N_MP = 8


def draw_krylov(key, part):
    key = jax.random.fold_in(key, 7)
    common_key, private_key = jax.random.split(key)
    shared = jax.random.truncated_normal(common_key, -4.0, 4.0, (D, FF), jnp.float32)
    private = jax.random.truncated_normal(private_key, -4.0, 4.0, (KRYLOV, D, FF), jnp.float32)
    mixing = 0.5
    strength = math.log(3.0)
    row_place = jnp.arange(D, dtype=jnp.float32) / D
    column_place = jnp.arange(FF, dtype=jnp.float32) / FF
    ramp = jnp.exp(strength * (row_place[:, None] + column_place[None, :]) - strength)
    mixed = math.sqrt(mixing) * shared[None] + math.sqrt(1.0 - mixing) * private
    return mixed * ramp[None]


def spiked(drawn, key, source, target, blocks, factor):
    def block_of(dim):
        return (jnp.arange(drawn.shape[dim]) // (drawn.shape[dim] // blocks)).reshape((-1,) + (1,) * (drawn.ndim - 1 - dim))

    first = jax.random.permutation(key, blocks)[block_of(target)]
    far = (block_of(target) + blocks // 2) % blocks
    return jnp.where((block_of(source) == first) | (block_of(source) == far), factor * drawn, drawn)


def steps_of(key, shape, pieces, smallest, high):
    gain, own = 1.0, jax.random.fold_in(key, 6)
    for axis_at, shards_of in pieces:
        draws = jnp.exp(jax.random.uniform(jax.random.fold_in(own, axis_at), (shards_of,), jnp.float32, smallest / len(pieces), high / len(pieces)))
        gain = gain * jnp.repeat(draws, shape[axis_at] // shards_of).reshape([-1 if axis == axis_at else 1 for axis in range(len(shape))])
    return gain


def normal_values(own_key, shape, scale, most, cuts=(), held_as=jnp.bfloat16):
    factor_of = steps_of(own_key, shape, cuts, -0.22, 0.18) if cuts else 1.0
    array = jax.random.normal(own_key, shape, jnp.float32) * scale * factor_of
    return jnp.minimum(jnp.maximum(array, -most), most).astype(held_as)


def gaussian_with(stream_key, shape, deviation, bound, cuts, heavy, held_as=jnp.bfloat16):
    entries = deviation * jax.random.normal(stream_key, shape, jnp.float32)
    if cuts:
        entries = entries * steps_of(stream_key, shape, cuts, -0.22, 0.18)
    return jnp.clip(spiked(entries, jax.random.fold_in(stream_key, 3), *heavy), -bound, bound).astype(held_as)


def setup_inputs(seed: int = 0) -> dict:
    keys = jax.random.split(jax.random.key(seed), 7)
    tokens = gaussian_with(keys[0], (TOKENS, D), 1.0, 6.0, ((0, 32),), (0, 1, 32, 2.75))
    targets = normal_values(keys[1], (TOKENS, D), 1.0, 6.0, ((0, 32),))
    gate_weight = normal_values(keys[2], (D, FF), D ** -0.5, 0.09375, ((0, 32), (1, 8)))
    up_weight = normal_values(keys[3], (D, FF), D ** -0.5, 0.09375, ((0, 32), (1, 8)))
    down_weight = normal_values(keys[4], (D, FF), FF ** -0.5, 0.078125, ((0, 32), (1, 8)))
    krylov = draw_krylov(jax.random.fold_in(keys[6], 71), 0)
    return dict(tokens=tokens, targets=targets, gate_weight=gate_weight, up_weight=up_weight, down_weight=down_weight, krylov=krylov)


root_scale = math.sqrt(2.0 / math.pi)
cubic_term = 0.044715
epsilon = 1e-06

def gelu_parts(values):
    inside = root_scale * (values + cubic_term * values * values * values)
    hyperbolic = jnp.tanh(inside)
    rising = root_scale * (1.0 + 3.0 * cubic_term * values * values)
    falloff = 1.0 - hyperbolic * hyperbolic
    result = 0.5 * values * (1.0 + hyperbolic)
    derivative = 0.5 * (1.0 + hyperbolic) + 0.5 * values * falloff * rising
    curvature = falloff * rising + 0.5 * values * falloff * (6.0 * root_scale * cubic_term * values - 2.0 * hyperbolic * rising * rising)
    return (result, derivative, curvature)

def normalize(tokens):
    values = tokens.astype(jnp.float32)
    inverse = lax.rsqrt(lax.optimization_barrier(jnp.mean(values * values, axis=1, keepdims=True)) + epsilon)
    return (values * inverse).astype(jnp.bfloat16)

def rounded(values):
    return lax.optimization_barrier(values.astype(jnp.bfloat16)).astype(jnp.float32)

def reference(tokens, targets, gate_weight, up_weight, down_weight, krylov):
    normed = normalize(tokens)
    direction = krylov[KRYLOV - 1].astype(jnp.bfloat16)
    gate = jnp.dot(normed, gate_weight, preferred_element_type=jnp.float32)
    upward = jnp.dot(normed, up_weight, preferred_element_type=jnp.float32)
    tangent = jnp.dot(normed, direction, preferred_element_type=jnp.float32)
    activated, derivative, curvature = gelu_parts(gate)
    hidden = (activated * upward).astype(jnp.bfloat16)
    hidden_tangent = (derivative * tangent * upward).astype(jnp.bfloat16)
    span = FF // N_MP
    outputs = jnp.zeros((TOKENS, D), jnp.float32)
    outputs_tangent = jnp.zeros((TOKENS, D), jnp.float32)
    for position in range(N_MP):
        down_part = down_weight[:, position * span:(position + 1) * span]
        hidden_part = hidden[:, position * span:(position + 1) * span]
        tangent_part = hidden_tangent[:, position * span:(position + 1) * span]
        outputs = outputs + rounded(jnp.dot(hidden_part, down_part.T, preferred_element_type=jnp.float32))
        outputs_tangent = outputs_tangent + rounded(jnp.dot(tangent_part, down_part.T, preferred_element_type=jnp.float32))
    residual = (tokens.astype(jnp.float32) + outputs - targets.astype(jnp.float32)).astype(jnp.bfloat16)
    residual_tangent = outputs_tangent.astype(jnp.bfloat16)
    backward = jnp.dot(residual, down_weight, preferred_element_type=jnp.float32)
    backward_tangent = jnp.dot(residual_tangent, down_weight, preferred_element_type=jnp.float32)
    gate_tangent = ((backward_tangent * derivative + backward * curvature * tangent) * upward).astype(jnp.bfloat16)
    product = jnp.zeros((D, FF), jnp.float32)
    for position in range(N_DP):
        normed_part = normed[position * TOK_DEV:(position + 1) * TOK_DEV]
        gate_part = gate_tangent[position * TOK_DEV:(position + 1) * TOK_DEV]
        term = lax.dot_general(normed_part, gate_part, (((0,), (0,)), ((), ())), preferred_element_type=jnp.float32)
        product = product + rounded(term)
    product = product / TOKENS
    projections = jnp.stack([jnp.sum(krylov[position] * product) for position in range(KRYLOV)]) / (D * FF)
    projected = product
    for position in range(KRYLOV):
        projected = projected - projections[position] * krylov[position]
    norm_value = jnp.sqrt(jnp.mean(projected * projected) + epsilon)
    next_vector = projected / norm_value
    coefficients = jnp.concatenate([projections, norm_value[None]])
    return (next_vector, coefficients)
```

```python
import math

import jax
import jax.numpy as jnp
from jax import lax
from jax.sharding import Mesh
from jax.sharding import PartitionSpec as P

KRYLOV = 4
NX, NZ, NY, NC = 4, 8, 4, 2

root_scale = math.sqrt(2.0 / math.pi)
cubic_term = 0.044715
epsilon = 1e-06

F32 = jnp.float32
BF16 = jnp.bfloat16


def gelu_parts(values):
    inside = root_scale * (values + cubic_term * values * values * values)
    hyperbolic = jnp.tanh(inside)
    rising = root_scale * (1.0 + 3.0 * cubic_term * values * values)
    falloff = 1.0 - hyperbolic * hyperbolic
    result = 0.5 * values * (1.0 + hyperbolic)
    derivative = 0.5 * (1.0 + hyperbolic) + 0.5 * values * falloff * rising
    curvature = falloff * rising + 0.5 * values * falloff * (
        6.0 * root_scale * cubic_term * values - 2.0 * hyperbolic * rising * rising
    )
    return (result, derivative, curvature)


def normalize(tokens):
    values = tokens.astype(F32)
    inverse = lax.rsqrt(jnp.mean(values * values, axis=1, keepdims=True) + epsilon)
    return (values * inverse).astype(BF16)


def contract(left, right, left_dim, right_dim):
    return lax.dot_general(
        left, right, (((left_dim,), (right_dim,)), ((), ())), preferred_element_type=F32
    )


def shift(value, axis, by):
    size = lax.axis_size(axis)
    return lax.ppermute(value, axis, [(i, (i + by) % size) for i in range(size)])


def rolled(value, dim, start):
    size = value.shape[dim]
    return lax.dynamic_slice_in_dim(jnp.concatenate([value, value], dim), start, size, dim)


def added(first, second):
    return (first.astype(F32) + second.astype(F32)).astype(BF16)


def added_front(whole, front):
    rows = front.shape[0]
    return jnp.concatenate([added(whole[:rows], front), whole[rows:]], 0)


def added_back(whole, back):
    rows = whole.shape[0] - back.shape[0]
    return jnp.concatenate([whole[:rows], added(whole[rows:], back)], 0)


def ring_sum(blocks, axis):
    size = len(blocks)
    far = size // 2
    half = blocks[far].shape[0] // 2
    ahead = shift(blocks[far][:half], axis, 1)
    behind = shift(blocks[far][half:], axis, -1)
    onward = added_front(blocks[far - 1], ahead)
    backward = added_back(blocks[far + 1], behind)
    for step in range(far - 1, 0, -1):
        ahead = shift(onward, axis, 1)
        behind = shift(backward, axis, -1)
        if step > 1:
            onward = added(blocks[step - 1], ahead)
            backward = added(blocks[size - step + 1], behind)
    return blocks[0].astype(F32) + ahead.astype(F32) + behind.astype(F32)


def ring_gather(own, axis):
    half = own.shape[0] // 2
    before = shift(own, axis, 1)
    after = shift(own, axis, -1)
    far = jnp.concatenate([shift(before[:half], axis, 1), shift(after[half:], axis, -1)], 0)
    return [own, after, far, before]


def total(value):
    for axis, size in (("c", NC), ("y", NY), ("x", NX), ("z", NZ)):
        stride = 1
        while stride < size:
            value = value + lax.ppermute(value, axis, [(i, i ^ stride) for i in range(size)])
            stride *= 2
    return value


def local(tokens, targets, gate_weight, up_weight, down_weight, krylov):
    rows, width = tokens.shape
    span = gate_weight.shape[1]
    depth = gate_weight.shape[0]
    own_rows = rows // (NY * NC)
    at_x, at_z, at_y, at_c = (lax.axis_index(name) for name in ("x", "z", "y", "c"))

    direction = krylov[KRYLOV - 1].astype(BF16)
    gathered = lax.all_gather(
        jnp.concatenate([gate_weight, up_weight, direction, down_weight], 1),
        ("x", "z"),
        axis=0,
        tiled=True,
    )
    down_full = gathered[:, 3 * span:]

    placed = jnp.swapaxes(tokens.reshape(NY, NC, own_rows, width), 0, 1)
    placed = rolled(rolled(placed, 0, at_c), 1, at_y)
    own_tokens = placed[0, 0]
    normed = normalize(placed.reshape(rows, width))
    own_targets = lax.dynamic_slice_in_dim(targets, (at_y * NC + at_c) * own_rows, own_rows, 0)
    turned = normed.T.reshape(NX, NZ, depth, rows)
    turned = rolled(rolled(turned, 0, at_x), 1, at_z)
    gram = jnp.sum(krylov[:, None] * krylov[None], axis=(2, 3)).reshape(-1)

    forward = jnp.dot(normed, gathered[:, : 3 * span], preferred_element_type=F32)
    gate, upward, tangent = jnp.split(forward, 3, axis=1)
    activated, derivative, curvature = gelu_parts(gate)
    hidden = (activated * upward).astype(BF16)
    hidden_tangent = (derivative * tangent * upward).astype(BF16)
    both = jnp.stack(
        [a.reshape(NC, NY, own_rows, span) for a in (hidden, hidden_tangent)], 2
    ).reshape(NC, NY * 2 * own_rows, span)

    theirs = shift(contract(both[1], down_full, 1, 1).astype(BF16), "c", 1)
    mine = added(contract(both[0], down_full, 1, 1).astype(BF16), theirs)
    mine = mine.reshape(NY, 2, own_rows, width)
    outputs, outputs_tangent = ring_sum([mine[d] for d in range(NY)], "y")
    residual = (own_tokens.astype(F32) + outputs - own_targets.astype(F32)).astype(BF16)
    residuals = jnp.stack([residual, outputs_tangent.astype(BF16)], 0)
    chip = jnp.stack(ring_gather(residuals, "y"), 0).reshape(NY * 2 * own_rows, width)
    other = shift(chip, "c", 1)
    backs = jnp.stack(
        [
            jnp.dot(part, down_full, preferred_element_type=F32).reshape(NY, 2, own_rows, span)
            for part in (chip, other)
        ],
        0,
    )
    backward = backs[:, :, 0].reshape(rows, span)
    backward_tangent = backs[:, :, 1].reshape(rows, span)
    gate_tangent = (
        (backward_tangent * derivative + backward * curvature * tangent) * upward
    ).astype(BF16)

    cut = span * 3 // 5
    first, second = gate_tangent[:, :cut], gate_tangent[:, cut:]
    blocks = [
        contract(turned[d].reshape(NZ * depth, rows), first, 1, 0).astype(BF16)
        for d in range(NX)
    ]
    by_x = ring_sum(blocks, "x").astype(BF16).reshape(NZ, depth, cut)
    left = ring_sum([by_x[d] for d in range(NZ)], "z")
    blocks = [
        contract(turned[:, d].reshape(NX * depth, rows), second, 1, 0).astype(BF16)
        for d in range(NZ)
    ]
    by_z = ring_sum(blocks, "z").astype(BF16).reshape(NX, depth, span - cut)
    right = ring_sum([by_z[d] for d in range(NX)], "x")

    tokens_in_all = rows * NX * NZ
    product = jnp.concatenate([left, right], 1) / tokens_in_all
    entries = depth * NX * NZ * span * NY * NC
    scaled = product / 4096.0
    sums = jnp.concatenate(
        [
            jnp.sum(krylov * product[None], axis=(1, 2)),
            gram,
            jnp.sum(scaled * scaled).reshape(1),
        ]
    )
    sums = total(sums)
    projections = sums[:KRYLOV] / entries
    grams = sums[KRYLOV : KRYLOV + KRYLOV * KRYLOV].reshape(KRYLOV, KRYLOV) / entries
    mean_product = sums[-1] * (4096.0 * 4096.0 / entries)
    mean_square = (
        mean_product
        - 2.0 * jnp.sum(projections * projections)
        + jnp.sum(projections[:, None] * projections[None] * grams)
    )
    norm_value = jnp.sqrt(jnp.maximum(mean_square, 0.0) + epsilon)
    projected = product - jnp.sum(projections[:, None, None] * krylov, axis=0)
    next_vector = projected / norm_value
    coefficients = jnp.concatenate([projections, jnp.reshape(norm_value, (1,))])
    return (next_vector, coefficients)


def solution(mesh):
    split = Mesh(mesh.devices.reshape(NX, NZ, NY, NC), ("x", "z", "y", "c"))
    dp, mp = ("x", "z"), ("y", "c")
    placed = (
        P(dp, None),
        P(dp, None),
        P(dp, mp),
        P(dp, mp),
        P(dp, mp),
        P(None, dp, mp),
    )
    return jax.shard_map(
        local, mesh=split, in_specs=placed, out_specs=(P(dp, mp), P()), check_vma=False
    )
```

```python
import math

import jax
import jax.numpy as jnp
from jax import lax
from jax.sharding import Mesh
from jax.sharding import PartitionSpec as P

KRYLOV = 4
NX, NZ, NY, NC = 4, 8, 4, 2

root_scale = math.sqrt(2.0 / math.pi)
cubic_term = 0.044715
epsilon = 1e-06

F32 = jnp.float32
BF16 = jnp.bfloat16


def gelu_parts(values):
    inside = root_scale * (values + cubic_term * values * values * values)
    hyperbolic = jnp.tanh(inside)
    rising = root_scale * (1.0 + 3.0 * cubic_term * values * values)
    falloff = 1.0 - hyperbolic * hyperbolic
    result = 0.5 * values * (1.0 + hyperbolic)
    derivative = 0.5 * (1.0 + hyperbolic) + 0.5 * values * falloff * rising
    curvature = falloff * rising + 0.5 * values * falloff * (
        6.0 * root_scale * cubic_term * values - 2.0 * hyperbolic * rising * rising
    )
    return (result, derivative, curvature)


def normalize(tokens):
    values = tokens.astype(F32)
    inverse = lax.rsqrt(jnp.mean(values * values, axis=1, keepdims=True) + epsilon)
    return (values * inverse).astype(BF16)


def contract(left, right, left_dim, right_dim):
    return lax.dot_general(
        left, right, (((left_dim,), (right_dim,)), ((), ())), preferred_element_type=F32
    )


def shift(value, axis, by):
    size = lax.axis_size(axis)
    return lax.ppermute(value, axis, [(i, (i + by) % size) for i in range(size)])


def rolled(value, dim, start):
    size = value.shape[dim]
    return lax.dynamic_slice_in_dim(jnp.concatenate([value, value], dim), start, size, dim)


def added(first, second):
    return (first.astype(F32) + second.astype(F32)).astype(BF16)


def added_front(whole, front):
    rows = front.shape[0]
    return jnp.concatenate([added(whole[:rows], front), whole[rows:]], 0)


def added_back(whole, back):
    rows = whole.shape[0] - back.shape[0]
    return jnp.concatenate([whole[:rows], added(whole[rows:], back)], 0)


def ring_sum(blocks, axis):
    size = len(blocks)
    far = size // 2
    half = blocks[far].shape[0] // 2
    ahead = shift(blocks[far][:half], axis, 1)
    behind = shift(blocks[far][half:], axis, -1)
    onward = added_front(blocks[far - 1], ahead)
    backward = added_back(blocks[far + 1], behind)
    for step in range(far - 1, 0, -1):
        ahead = shift(onward, axis, 1)
        behind = shift(backward, axis, -1)
        if step > 1:
            onward = added(blocks[step - 1], ahead)
            backward = added(blocks[size - step + 1], behind)
    return blocks[0].astype(F32) + ahead.astype(F32) + behind.astype(F32)


def ring_gather(own, axis):
    far = lax.axis_size(axis) // 2
    half = own.shape[0] // 2
    before, after = [own], [own]
    for _ in range(1, far):
        before.append(shift(before[-1], axis, 1))
        after.append(shift(after[-1], axis, -1))
    farthest = jnp.concatenate(
        [shift(before[-1][:half], axis, 1), shift(after[-1][half:], axis, -1)], 0
    )
    return after + [farthest] + before[:0:-1]


def spread(value, axes, size, strides):
    first, second, third = (
        lax.ppermute(value, axes, [(i, i ^ stride) for i in range(size)]) for stride in strides
    )
    return (value + first) + (second + third)


def total(value):
    value = spread(value, "y", NY, (1, 2, 3))
    value = spread(value, "x", NX, (1, 2, 3))
    value = spread(value, "z", NZ, (1, 2, 3))
    return spread(value, ("z", "c"), NZ * NC, (1, 8, 9))


def local(tokens, targets, gate_weight, up_weight, down_weight, krylov):
    rows, width = tokens.shape
    depth, span = gate_weight.shape
    own_rows = rows // (NY * NC)
    slab = width // NX
    at_x, at_z, at_y, at_c = (lax.axis_index(name) for name in ("x", "z", "y", "c"))
    near = [0, 1, NZ - 1]
    distant = [d for d in range(NZ) if d not in near]

    direction = krylov[KRYLOV - 1].astype(BF16)
    gathered = lax.all_gather(
        jnp.concatenate([gate_weight, up_weight, direction], 1), "z", axis=0, tiled=True
    )

    ring = ring_gather(down_weight, "z")
    near_rows = ring_gather(jnp.concatenate([ring[d] for d in near], 0), "x")
    distant_rows = ring_gather(jnp.concatenate([ring[d] for d in distant], 0), "x")
    down_full = lax.optimization_barrier(
        jnp.concatenate([part for d in range(NX) for part in (near_rows[d], distant_rows[d])], 0)
    )

    def arranged(values):
        values = values.reshape(own_rows, NX, NZ, depth)
        values = rolled(rolled(values, 1, at_x), 2, at_z)
        return jnp.stack([values[:, :, d] for d in near + distant], 2).reshape(own_rows, width)

    placed = jnp.swapaxes(tokens.reshape(NY, NC, own_rows, width), 0, 1)
    placed = rolled(rolled(placed, 0, at_c), 1, at_y)
    own_tokens = arranged(placed[0, 0])
    own_targets = arranged(
        lax.dynamic_slice_in_dim(targets, (at_y * NC + at_c) * own_rows, own_rows, 0)
    )
    normed = normalize(placed.reshape(rows, width))

    def features(ahead, count):
        start = lax.rem(at_x + ahead, NX) * slab
        return lax.dynamic_slice(normed, (0, start), (count, slab))

    half = rows // NC
    fetched = [shift(features(ahead, half), "x", ahead) for ahead in range(NX - 1, 0, -1)]
    fetched = jnp.stack(fetched, 0)
    fetched = jnp.concatenate([fetched, shift(fetched, "c", 1)], 1)
    around = jnp.concatenate([features(0, rows)[None], fetched], 0)
    turned = rolled(around.reshape(NX * rows, slab).T.reshape(NZ, depth, NX * rows), 0, at_z)
    gram = jnp.sum(krylov[:, None] * krylov[None], axis=(2, 3)).reshape(-1)
    turned, gram, own_tokens, own_targets = lax.optimization_barrier(
        (turned, gram, own_tokens, own_targets)
    )

    terms = {
        d: lax.optimization_barrier(
            jnp.dot(around[d], gathered, preferred_element_type=F32).astype(BF16)
        )
        for d in (2, 1, 3, 0)
    }
    forward = ring_sum([terms[d] for d in range(NX)], "x")
    gate, upward, tangent = jnp.split(forward, 3, axis=1)
    activated, derivative, curvature = gelu_parts(gate)
    hidden = (activated * upward).astype(BF16)
    hidden_tangent = (derivative * tangent * upward).astype(BF16)
    both = jnp.stack(
        [a.reshape(NC, NY, own_rows, span) for a in (hidden, hidden_tangent)], 2
    ).reshape(NC, NY * 2 * own_rows, span)

    theirs = shift(contract(both[1], down_full, 1, 1).astype(BF16), "c", 1)
    mine = lax.optimization_barrier(contract(both[0], down_full, 1, 1).astype(BF16))
    mine = added(mine, theirs).reshape(NY, 2, own_rows, width)
    outputs, outputs_tangent = ring_sum([mine[d] for d in range(NY)], "y")
    residual = (own_tokens.astype(F32) + outputs - own_targets.astype(F32)).astype(BF16)
    residuals = jnp.stack([residual, outputs_tangent.astype(BF16)], 0)
    chip = jnp.stack(ring_gather(residuals, "y"), 0).reshape(NY * 2 * own_rows, width)
    other = shift(chip, "c", 1)
    backs = jnp.stack(
        [
            jnp.dot(part, down_full, preferred_element_type=F32).reshape(NY, 2, own_rows, span)
            for part in (chip, other)
        ],
        0,
    )
    backward = backs[:, :, 0].reshape(rows, span)
    backward_tangent = backs[:, :, 1].reshape(rows, span)
    gate_tangent = (
        (backward_tangent * derivative + backward * curvature * tangent) * upward
    ).astype(BF16)

    every = jnp.concatenate(ring_gather(gate_tangent, "x"), 0)
    blocks = [
        lax.optimization_barrier(contract(turned[d], every, 1, 0).astype(BF16))
        for d in range(NZ)
    ]
    product = ring_sum(blocks, "z") / (rows * NX * NZ)

    entries = width * span * NY * NC
    scaled = product / 4096.0
    sums = jnp.concatenate(
        [
            jnp.sum(krylov * product[None], axis=(1, 2)),
            gram,
            jnp.sum(scaled * scaled).reshape(1),
        ]
    )
    sums = total(sums)
    projections = sums[:KRYLOV] / entries
    grams = sums[KRYLOV : KRYLOV + KRYLOV * KRYLOV].reshape(KRYLOV, KRYLOV) / entries
    mean_product = sums[-1] * (4096.0 * 4096.0 / entries)
    mean_square = (
        mean_product
        - 2.0 * jnp.sum(projections * projections)
        + jnp.sum(projections[:, None] * projections[None] * grams)
    )
    norm_value = jnp.sqrt(jnp.maximum(mean_square, 0.0) + epsilon)
    projected = product - jnp.sum(projections[:, None, None] * krylov, axis=0)
    next_vector = projected / norm_value
    coefficients = jnp.concatenate([projections, jnp.reshape(norm_value, (1,))])
    return (next_vector, coefficients)


def solution(mesh):
    split = Mesh(mesh.devices.reshape(NX, NZ, NY, NC), ("x", "z", "y", "c"))
    dp, mp = ("x", "z"), ("y", "c")
    placed = (
        P(dp, None),
        P(dp, None),
        P(dp, mp),
        P(dp, mp),
        P(dp, mp),
        P(None, dp, mp),
    )
    return jax.shard_map(
        local, mesh=split, in_specs=placed, out_specs=(P(dp, mp), P()), check_vma=False
    )
```

```python
import math

import jax
import jax.numpy as jnp
from jax import lax
from jax.sharding import Mesh
from jax.sharding import PartitionSpec as P

KRYLOV = 4
NX, NZ, NY, NC = 4, 8, 4, 2

root_scale = math.sqrt(2.0 / math.pi)
cubic_term = 0.044715
epsilon = 1e-06

F32 = jnp.float32
BF16 = jnp.bfloat16


def gelu_parts(values):
    inside = root_scale * (values + cubic_term * values * values * values)
    hyperbolic = jnp.tanh(inside)
    rising = root_scale * (1.0 + 3.0 * cubic_term * values * values)
    falloff = 1.0 - hyperbolic * hyperbolic
    result = 0.5 * values * (1.0 + hyperbolic)
    derivative = 0.5 * (1.0 + hyperbolic) + 0.5 * values * falloff * rising
    curvature = falloff * rising + 0.5 * values * falloff * (
        6.0 * root_scale * cubic_term * values - 2.0 * hyperbolic * rising * rising
    )
    return (result, derivative, curvature)


def normalize(tokens):
    values = tokens.astype(F32)
    inverse = lax.rsqrt(jnp.mean(values * values, axis=1, keepdims=True) + epsilon)
    return (values * inverse).astype(BF16)


def contract(left, right, left_dim, right_dim):
    return lax.dot_general(
        left, right, (((left_dim,), (right_dim,)), ((), ())), preferred_element_type=F32
    )


def shift(value, axis, by):
    size = lax.axis_size(axis)
    return lax.ppermute(value, axis, [(i, (i + by) % size) for i in range(size)])


def rolled(value, dim, start):
    size = value.shape[dim]
    return lax.dynamic_slice_in_dim(jnp.concatenate([value, value], dim), start, size, dim)


def added(first, second):
    return (first.astype(F32) + second.astype(F32)).astype(BF16)


def added_front(whole, front):
    return lax.dynamic_update_slice_in_dim(whole, added(whole[: front.shape[0]], front), 0, 0)


def added_back(whole, back):
    rows = whole.shape[0] - back.shape[0]
    return lax.dynamic_update_slice_in_dim(whole, added(whole[rows:], back), rows, 0)


def ring_sum(blocks, axis):
    size = len(blocks)
    far = size // 2
    half = blocks[far].shape[0] // 2
    ahead = shift(blocks[far][:half], axis, 1)
    behind = shift(blocks[far][half:], axis, -1)
    onward = added_front(blocks[far - 1], ahead)
    backward = added_back(blocks[far + 1], behind)
    for step in range(far - 1, 0, -1):
        ahead = shift(onward, axis, 1)
        behind = shift(backward, axis, -1)
        if step > 1:
            onward = added(blocks[step - 1], ahead)
            backward = added(blocks[size - step + 1], behind)
    return blocks[0].astype(F32) + ahead.astype(F32) + behind.astype(F32)


def ring_gather(own, axis):
    far = lax.axis_size(axis) // 2
    half = own.shape[0] // 2
    before, after = [own], [own]
    for _ in range(1, far):
        before.append(shift(before[-1], axis, 1))
        after.append(shift(after[-1], axis, -1))
    farthest = jnp.concatenate(
        [shift(before[-1][:half], axis, 1), shift(after[-1][half:], axis, -1)], 0
    )
    return after + [farthest] + before[:0:-1]


def total(value):
    devices = NX * NZ * NY * NC
    mine = jnp.zeros((128,), F32).at[: value.shape[0]].set(value)
    every = lax.all_to_all(
        jnp.broadcast_to(mine, (devices, 128)), ("x", "z", "y", "c"), 0, 0, tiled=True
    )
    return jnp.sum(every, axis=0)[: value.shape[0]]


def local(tokens, targets, gate_weight, up_weight, down_weight, krylov):
    rows, width = tokens.shape
    depth, span = gate_weight.shape
    own_rows = rows // (NY * NC)
    slab = width // NX
    at_x, at_z, at_y, at_c = (lax.axis_index(name) for name in ("x", "z", "y", "c"))

    direction = krylov[KRYLOV - 1].astype(BF16)
    gathered = lax.all_gather(
        jnp.concatenate([gate_weight, up_weight, direction], 1), "z", axis=0, tiled=True
    )

    across = jnp.concatenate(ring_gather(down_weight, "x"), 0)
    down_full = lax.all_gather(across, "z", axis=0, tiled=True)

    def arranged(values):
        values = rolled(values.reshape(own_rows, NX, NZ, depth), 1, at_x)
        return jnp.swapaxes(values, 1, 2).reshape(own_rows, width)

    placed = jnp.swapaxes(tokens.reshape(NY, NC, own_rows, width), 0, 1)
    placed = rolled(rolled(placed, 0, at_c), 1, at_y)
    own_tokens = arranged(placed[0, 0])
    own_targets = arranged(
        lax.dynamic_slice_in_dim(targets, (at_y * NC + at_c) * own_rows, own_rows, 0)
    )
    normed = normalize(placed.reshape(rows, width))

    def features(ahead, count):
        start = lax.rem(at_x + ahead, NX) * slab
        return lax.dynamic_slice(normed, (0, start), (count, slab))

    half = rows // NC
    fetched = [shift(features(ahead, half), "x", ahead) for ahead in range(NX - 1, 0, -1)]
    fetched = jnp.stack(fetched, 0)
    fetched = jnp.concatenate([fetched, shift(fetched, "c", 1)], 1)
    around = jnp.concatenate([features(0, rows)[None], fetched], 0)
    turned = rolled(around.reshape(NX * rows, slab).T.reshape(NZ, depth, NX * rows), 0, at_z)
    gram = jnp.sum(krylov[:, None] * krylov[None], axis=(2, 3)).reshape(-1)
    turned, gram, own_tokens, own_targets = lax.optimization_barrier(
        (turned, gram, own_tokens, own_targets)
    )

    terms = {
        d: lax.optimization_barrier(
            jnp.dot(around[d], gathered, preferred_element_type=F32).astype(BF16)
        )
        for d in (2, 1, 3, 0)
    }
    forward = ring_sum([terms[d] for d in range(NX)], "x")
    gate, upward, tangent = jnp.split(forward, 3, axis=1)
    activated, derivative, curvature = gelu_parts(gate)
    hidden = (activated * upward).astype(BF16)
    hidden_tangent = (derivative * tangent * upward).astype(BF16)
    both = jnp.stack(
        [a.reshape(NC, NY, own_rows, span) for a in (hidden, hidden_tangent)], 2
    ).reshape(NC, NY * 2 * own_rows, span)

    theirs = shift(contract(both[1], down_full, 1, 1).astype(BF16), "c", 1)
    mine = lax.optimization_barrier(contract(both[0], down_full, 1, 1).astype(BF16))
    mine, theirs = (a.reshape(NY, 2, own_rows, width) for a in (mine, theirs))
    outputs, outputs_tangent = ring_sum([added(mine[d], theirs[d]) for d in range(NY)], "y")
    residual = (own_tokens.astype(F32) + outputs - own_targets.astype(F32)).astype(BF16)
    residuals = jnp.stack([residual, outputs_tangent.astype(BF16)], 0)
    chip = jnp.stack(ring_gather(residuals, "y"), 0).reshape(NY * 2 * own_rows, width)
    other = shift(chip, "c", 1)
    backs = jnp.stack(
        [
            jnp.dot(part, down_full, preferred_element_type=F32).reshape(NY, 2, own_rows, span)
            for part in (chip, other)
        ],
        0,
    )
    backward = backs[:, :, 0].reshape(rows, span)
    backward_tangent = backs[:, :, 1].reshape(rows, span)
    gate_tangent = (
        (backward_tangent * derivative + backward * curvature * tangent) * upward
    ).astype(BF16)

    every = jnp.concatenate(ring_gather(gate_tangent, "x"), 0)
    blocks = [
        lax.optimization_barrier(contract(turned[d], every, 1, 0).astype(BF16))
        for d in range(NZ)
    ]
    product = ring_sum(blocks, "z") / (rows * NX * NZ)

    entries = width * span * NY * NC
    scaled = product / 4096.0
    sums = jnp.concatenate(
        [
            jnp.sum(krylov * product[None], axis=(1, 2)),
            gram,
            jnp.sum(scaled * scaled).reshape(1),
        ]
    )
    sums = total(sums)
    projections = sums[:KRYLOV] / entries
    grams = sums[KRYLOV : KRYLOV + KRYLOV * KRYLOV].reshape(KRYLOV, KRYLOV) / entries
    mean_product = sums[-1] * (4096.0 * 4096.0 / entries)
    mean_square = (
        mean_product
        - 2.0 * jnp.sum(projections * projections)
        + jnp.sum(projections[:, None] * projections[None] * grams)
    )
    norm_value = jnp.sqrt(jnp.maximum(mean_square, 0.0) + epsilon)
    projected = product - jnp.sum(projections[:, None, None] * krylov, axis=0)
    next_vector = projected / norm_value
    coefficients = jnp.concatenate([projections, jnp.reshape(norm_value, (1,))])
    return (next_vector, coefficients)


def solution(mesh):
    split = Mesh(mesh.devices.reshape(NX, NZ, NY, NC), ("x", "z", "y", "c"))
    dp, mp = ("x", "z"), ("y", "c")
    placed = (
        P(dp, None),
        P(dp, None),
        P(dp, mp),
        P(dp, mp),
        P(dp, mp),
        P(None, dp, mp),
    )
    return jax.shard_map(
        local, mesh=split, in_specs=placed, out_specs=(P(dp, mp), P()), check_vma=False
    )
```

```python
import math

import jax
import jax.numpy as jnp
from jax import lax
from jax.sharding import Mesh
from jax.sharding import PartitionSpec as P

KRYLOV = 4
NX, NZ, NY, NC = 4, 8, 4, 2

root_scale = math.sqrt(2.0 / math.pi)
cubic_term = 0.044715
epsilon = 1e-06

F32 = jnp.float32
BF16 = jnp.bfloat16


def gelu_parts(values):
    inside = root_scale * (values + cubic_term * values * values * values)
    hyperbolic = jnp.tanh(inside)
    rising = root_scale * (1.0 + 3.0 * cubic_term * values * values)
    falloff = 1.0 - hyperbolic * hyperbolic
    result = 0.5 * values * (1.0 + hyperbolic)
    derivative = 0.5 * (1.0 + hyperbolic) + 0.5 * values * falloff * rising
    curvature = falloff * rising + 0.5 * values * falloff * (
        6.0 * root_scale * cubic_term * values - 2.0 * hyperbolic * rising * rising
    )
    return (result, derivative, curvature)


def normalize(tokens):
    values = tokens.astype(F32)
    inverse = lax.rsqrt(jnp.mean(values * values, axis=1, keepdims=True) + epsilon)
    return (values * inverse).astype(BF16)


def contract(left, right, left_dim, right_dim):
    return lax.dot_general(
        left, right, (((left_dim,), (right_dim,)), ((), ())), preferred_element_type=F32
    )


def shift(value, axis, by):
    size = lax.axis_size(axis)
    return lax.ppermute(value, axis, [(i, (i + by) % size) for i in range(size)])


def rolled(value, dim, start):
    size = value.shape[dim]
    return lax.dynamic_slice_in_dim(jnp.concatenate([value, value], dim), start, size, dim)


def added(first, second):
    return (first.astype(F32) + second.astype(F32)).astype(BF16)


def added_front(whole, front):
    return lax.dynamic_update_slice_in_dim(whole, added(whole[: front.shape[0]], front), 0, 0)


def added_back(whole, back):
    rows = whole.shape[0] - back.shape[0]
    return lax.dynamic_update_slice_in_dim(whole, added(whole[rows:], back), rows, 0)


def ring_sum(blocks, axis):
    size = len(blocks)
    far = size // 2
    half = blocks[far].shape[0] // 2
    ahead = shift(blocks[far][:half], axis, 1)
    behind = shift(blocks[far][half:], axis, -1)
    onward = added_front(blocks[far - 1], ahead)
    backward = added_back(blocks[far + 1], behind)
    for step in range(far - 1, 0, -1):
        ahead = shift(onward, axis, 1)
        behind = shift(backward, axis, -1)
        if step > 1:
            onward = added(blocks[step - 1], ahead)
            backward = added(blocks[size - step + 1], behind)
    return blocks[0].astype(F32) + ahead.astype(F32) + behind.astype(F32)


def ring_gather(own, axis):
    far = lax.axis_size(axis) // 2
    half = own.shape[0] // 2
    before, after = [own], [own]
    for _ in range(1, far):
        before.append(shift(before[-1], axis, 1))
        after.append(shift(after[-1], axis, -1))
    farthest = jnp.concatenate(
        [shift(before[-1][:half], axis, 1), shift(after[-1][half:], axis, -1)], 0
    )
    return after + [farthest] + before[:0:-1]


def total(value):
    devices = NX * NZ * NY * NC
    mine = jnp.zeros((128,), F32).at[: value.shape[0]].set(value)
    every = lax.all_to_all(
        jnp.broadcast_to(mine, (devices, 128)), ("x", "z", "y", "c"), 0, 0, tiled=True
    )
    return jnp.sum(every, axis=0)[: value.shape[0]]


def local(tokens, targets, gate_weight, up_weight, down_weight, krylov):
    rows, width = tokens.shape
    depth, span = gate_weight.shape
    own_rows = rows // (NY * NC)
    slab = width // NX
    at_x, at_z, at_y, at_c = (lax.axis_index(name) for name in ("x", "z", "y", "c"))

    gathered = lax.all_gather(
        jnp.concatenate([gate_weight, up_weight], 1), "z", axis=0, tiled=True
    )
    direction = krylov[KRYLOV - 1].astype(BF16)
    parts = ring_gather(direction, "z")
    direction = jnp.zeros((slab, span), BF16)
    for ahead in range(NZ):
        start = lax.rem(at_z + ahead, NZ) * depth
        direction = lax.dynamic_update_slice(direction, parts[ahead], (start, 0))

    across = jnp.concatenate(ring_gather(down_weight, "x"), 0)
    down_full = lax.all_gather(across, "z", axis=0, tiled=True)

    def arranged(values):
        values = rolled(values.reshape(own_rows, NX, NZ, depth), 1, at_x)
        return jnp.swapaxes(values, 1, 2).reshape(own_rows, width)

    placed = jnp.swapaxes(tokens.reshape(NY, NC, own_rows, width), 0, 1)
    placed = rolled(rolled(placed, 0, at_c), 1, at_y)
    own_tokens = arranged(placed[0, 0])
    own_targets = arranged(
        lax.dynamic_slice_in_dim(targets, (at_y * NC + at_c) * own_rows, own_rows, 0)
    )
    normed = normalize(placed.reshape(rows, width))

    def features(ahead, count):
        start = lax.rem(at_x + ahead, NX) * slab
        return lax.dynamic_slice(normed, (0, start), (count, slab))

    half = rows // NC
    fetched = [shift(features(ahead, half), "x", ahead) for ahead in range(NX - 1, 0, -1)]
    fetched = jnp.stack(fetched, 0)
    fetched = jnp.concatenate([fetched, shift(fetched, "c", 1)], 1)
    around = jnp.concatenate([features(0, rows)[None], fetched], 0)
    turned = rolled(around.reshape(NX * rows, slab).T.reshape(NZ, depth, NX * rows), 0, at_z)
    gram = jnp.sum(krylov[:, None] * krylov[None], axis=(2, 3)).reshape(-1)
    gathered, direction, around, turned, gram, own_tokens, own_targets = lax.optimization_barrier(
        (gathered, direction, around, turned, gram, own_tokens, own_targets)
    )
    matrices = lax.optimization_barrier(jnp.concatenate([gathered, direction], 1))

    terms = {
        d: lax.optimization_barrier(
            jnp.dot(around[d], matrices, preferred_element_type=F32).astype(BF16)
        )
        for d in (2, 1, 3, 0)
    }
    forward = ring_sum([terms[d] for d in range(NX)], "x")
    gate, upward, tangent = jnp.split(forward, 3, axis=1)
    activated, derivative, curvature = gelu_parts(gate)
    hidden = (activated * upward).astype(BF16)
    hidden_tangent = (derivative * tangent * upward).astype(BF16)
    both = jnp.stack(
        [a.reshape(NC, NY, own_rows, span) for a in (hidden, hidden_tangent)], 2
    ).reshape(NC, NY * 2 * own_rows, span)

    theirs = shift(contract(both[1], down_full, 1, 1).astype(BF16), "c", 1)
    mine = lax.optimization_barrier(contract(both[0], down_full, 1, 1).astype(BF16))
    mine, theirs = (a.reshape(NY, 2, own_rows, width) for a in (mine, theirs))
    outputs, outputs_tangent = ring_sum([added(mine[d], theirs[d]) for d in range(NY)], "y")
    residual = (own_tokens.astype(F32) + outputs - own_targets.astype(F32)).astype(BF16)
    residuals = jnp.stack([residual, outputs_tangent.astype(BF16)], 0)
    chip = jnp.stack(ring_gather(residuals, "y"), 0).reshape(NY * 2 * own_rows, width)
    other = shift(chip, "c", 1)
    backs = jnp.stack(
        [
            jnp.dot(part, down_full, preferred_element_type=F32).reshape(NY, 2, own_rows, span)
            for part in (chip, other)
        ],
        0,
    )
    backward = backs[:, :, 0].reshape(rows, span)
    backward_tangent = backs[:, :, 1].reshape(rows, span)
    gate_tangent = (
        (backward_tangent * derivative + backward * curvature * tangent) * upward
    ).astype(BF16)

    every = jnp.concatenate(ring_gather(gate_tangent, "x"), 0)
    blocks = [
        lax.optimization_barrier(contract(turned[d], every, 1, 0).astype(BF16))
        for d in range(NZ)
    ]
    product = ring_sum(blocks, "z") / (rows * NX * NZ)

    entries = width * span * NY * NC
    scaled = product / 4096.0
    sums = jnp.concatenate(
        [
            jnp.sum(krylov * product[None], axis=(1, 2)),
            gram,
            jnp.sum(scaled * scaled).reshape(1),
        ]
    )
    sums = total(sums)
    projections = sums[:KRYLOV] / entries
    grams = sums[KRYLOV : KRYLOV + KRYLOV * KRYLOV].reshape(KRYLOV, KRYLOV) / entries
    mean_product = sums[-1] * (4096.0 * 4096.0 / entries)
    mean_square = (
        mean_product
        - 2.0 * jnp.sum(projections * projections)
        + jnp.sum(projections[:, None] * projections[None] * grams)
    )
    norm_value = jnp.sqrt(jnp.maximum(mean_square, 0.0) + epsilon)
    projected = product - jnp.sum(projections[:, None, None] * krylov, axis=0)
    next_vector = projected / norm_value
    coefficients = jnp.concatenate([projections, jnp.reshape(norm_value, (1,))])
    return (next_vector, coefficients)


def solution(mesh):
    split = Mesh(mesh.devices.reshape(NX, NZ, NY, NC), ("x", "z", "y", "c"))
    dp, mp = ("x", "z"), ("y", "c")
    placed = (
        P(dp, None),
        P(dp, None),
        P(dp, mp),
        P(dp, mp),
        P(dp, mp),
        P(None, dp, mp),
    )
    return jax.shard_map(
        local, mesh=split, in_specs=placed, out_specs=(P(dp, mp), P()), check_vma=False
    )
```

```python
import math

import jax
import jax.numpy as jnp
from jax import lax
from jax.sharding import Mesh
from jax.sharding import PartitionSpec as P

KRYLOV = 4
NX, NZ, NY, NC = 4, 8, 4, 2

root_scale = math.sqrt(2.0 / math.pi)
cubic_term = 0.044715
epsilon = 1e-06

F32 = jnp.float32
BF16 = jnp.bfloat16


def gelu_parts(values):
    inside = root_scale * (values + cubic_term * values * values * values)
    hyperbolic = jnp.tanh(inside)
    rising = root_scale * (1.0 + 3.0 * cubic_term * values * values)
    falloff = 1.0 - hyperbolic * hyperbolic
    result = 0.5 * values * (1.0 + hyperbolic)
    derivative = 0.5 * (1.0 + hyperbolic) + 0.5 * values * falloff * rising
    curvature = falloff * rising + 0.5 * values * falloff * (
        6.0 * root_scale * cubic_term * values - 2.0 * hyperbolic * rising * rising
    )
    return (result, derivative, curvature)


def normalize(tokens):
    values = tokens.astype(F32)
    inverse = lax.rsqrt(jnp.mean(values * values, axis=1, keepdims=True) + epsilon)
    return (values * inverse).astype(BF16)


def contract(left, right, left_dim, right_dim):
    return lax.dot_general(
        left, right, (((left_dim,), (right_dim,)), ((), ())), preferred_element_type=F32
    )


def shift(value, axis, by):
    size = lax.axis_size(axis)
    return lax.ppermute(value, axis, [(i, (i + by) % size) for i in range(size)])


def rolled(value, dim, start):
    size = value.shape[dim]
    return lax.dynamic_slice_in_dim(jnp.concatenate([value, value], dim), start, size, dim)


def added(first, second):
    return (first.astype(F32) + second.astype(F32)).astype(BF16)


def added_front(whole, front):
    return lax.dynamic_update_slice_in_dim(whole, added(whole[: front.shape[0]], front), 0, 0)


def added_back(whole, back):
    rows = whole.shape[0] - back.shape[0]
    return lax.dynamic_update_slice_in_dim(whole, added(whole[rows:], back), rows, 0)


def ring_sum(blocks, axis):
    size = len(blocks)
    far = size // 2
    half = blocks[far].shape[0] // 2
    ahead = shift(blocks[far][:half], axis, 1)
    behind = shift(blocks[far][half:], axis, -1)
    onward = added_front(blocks[far - 1], ahead)
    backward = added_back(blocks[far + 1], behind)
    for step in range(far - 1, 0, -1):
        ahead = shift(onward, axis, 1)
        behind = shift(backward, axis, -1)
        if step > 1:
            onward = added(blocks[step - 1], ahead)
            backward = added(blocks[size - step + 1], behind)
    return blocks[0].astype(F32) + ahead.astype(F32) + behind.astype(F32)


def ring_gather(own, axis):
    far = lax.axis_size(axis) // 2
    half = own.shape[0] // 2
    before, after = [own], [own]
    for _ in range(1, far):
        before.append(shift(before[-1], axis, 1))
        after.append(shift(after[-1], axis, -1))
    farthest = jnp.concatenate(
        [shift(before[-1][:half], axis, 1), shift(after[-1][half:], axis, -1)], 0
    )
    return after + [farthest] + before[:0:-1]


def total(value):
    devices = NX * NZ * NY * NC
    mine = jnp.zeros((128,), F32).at[: value.shape[0]].set(value)
    every = lax.all_to_all(
        jnp.broadcast_to(mine, (devices, 128)), ("x", "z", "y", "c"), 0, 0, tiled=True
    )
    return jnp.sum(every, axis=0)[: value.shape[0]]


def local(tokens, targets, gate_weight, up_weight, down_weight, krylov):
    rows, width = tokens.shape
    depth, span = gate_weight.shape
    own_rows = rows // (NY * NC)
    slab = width // NX
    at_x, at_z, at_y, at_c = (lax.axis_index(name) for name in ("x", "z", "y", "c"))

    gathered = lax.all_gather(
        jnp.concatenate([gate_weight, up_weight], 1), "z", axis=0, tiled=True
    )
    direction = krylov[KRYLOV - 1].astype(BF16)
    before, after = [direction], [direction]
    before.append(shift(direction, "z", 1))
    after.append(shift(direction, "z", -1))
    down_before, down_after = shift(down_weight, "x", 1), shift(down_weight, "x", -1)

    normed = normalize(tokens).reshape(NY, NC, own_rows, width)
    normed = rolled(rolled(jnp.swapaxes(normed, 0, 1), 0, at_c), 1, at_y).reshape(rows, width)
    before[1], after[1], down_before, down_after, normed = lax.optimization_barrier(
        (before[1], after[1], down_before, down_after, normed)
    )

    def features(ahead, count):
        start = lax.rem(at_x + ahead, NX) * slab
        return lax.dynamic_slice(normed, (0, start), (count, slab))

    half = rows // NC
    fetched = [shift(features(ahead, half), "x", ahead) for ahead in range(NX - 1, 0, -1)]
    before.append(shift(before[1], "z", 1))
    after.append(shift(after[1], "z", -1))
    middle = depth // 2
    down_far = [shift(down_before[:middle], "x", 1), shift(down_after[middle:], "x", -1)]
    before[2], after[2], fetched, down_far = lax.optimization_barrier(
        (before[2], after[2], fetched, down_far)
    )

    across = jnp.concatenate([down_weight, down_after, *down_far, down_before], 0)
    down_full = lax.all_gather(across, "z", axis=0, tiled=True)

    before.append(shift(before[2], "z", 1))
    after.append(shift(after[2], "z", -1))
    fetched = jnp.stack(fetched, 0)
    fetched = jnp.concatenate([fetched, shift(fetched, "c", 1)], 1)
    around = jnp.concatenate([features(0, rows)[None], fetched], 0)
    far = [shift(before[3][:middle], "z", 1), shift(after[3][middle:], "z", -1)]
    parts = after + [jnp.concatenate(far, 0)] + before[:0:-1]
    direction = jnp.zeros((slab, span), BF16)
    for ahead in range(NZ):
        start = lax.rem(at_z + ahead, NZ) * depth
        direction = lax.dynamic_update_slice(direction, parts[ahead], (start, 0))

    def arranged(values):
        values = rolled(values.reshape(own_rows, NX, NZ, depth), 1, at_x)
        return jnp.swapaxes(values, 1, 2).reshape(own_rows, width)

    place = (at_y * NC + at_c) * own_rows
    own_tokens, own_targets = (
        arranged(lax.dynamic_slice_in_dim(a, place, own_rows, 0)) for a in (tokens, targets)
    )
    turned = rolled(around.reshape(NX * rows, slab).T.reshape(NZ, depth, NX * rows), 0, at_z)
    gram = jnp.sum(krylov[:, None] * krylov[None], axis=(2, 3)).reshape(-1)
    gathered, direction, around = lax.optimization_barrier((gathered, direction, around))
    matrices = jnp.concatenate([gathered, direction], 1)
    terms = lax.optimization_barrier(
        [
            jnp.dot(around[d], matrices, preferred_element_type=F32).astype(BF16)
            for d in range(NX)
        ]
    )
    forward = ring_sum(terms, "x")
    gate, upward, tangent = jnp.split(forward, 3, axis=1)
    activated, derivative, curvature = gelu_parts(gate)
    hidden = (activated * upward).astype(BF16)
    hidden_tangent = (derivative * tangent * upward).astype(BF16)
    both = jnp.stack(
        [a.reshape(NC, NY, own_rows, span) for a in (hidden, hidden_tangent)], 2
    ).reshape(NC, NY * 2 * own_rows, span)

    both, down_full, turned, gram, own_tokens, own_targets = lax.optimization_barrier(
        (both, down_full, turned, gram, own_tokens, own_targets)
    )

    theirs = shift(contract(both[1], down_full, 1, 1).astype(BF16), "c", 1)
    mine = lax.optimization_barrier(contract(both[0], down_full, 1, 1).astype(BF16))
    mine, theirs = (a.reshape(NY, 2, own_rows, width) for a in (mine, theirs))
    mine = lax.optimization_barrier([added(mine[d], theirs[d]) for d in range(NY)])
    outputs, outputs_tangent = ring_sum(mine, "y")
    residual = (own_tokens.astype(F32) + outputs - own_targets.astype(F32)).astype(BF16)
    residuals = jnp.stack([residual, outputs_tangent.astype(BF16)], 0)
    chip = jnp.stack(ring_gather(residuals, "y"), 0).reshape(NY * 2 * own_rows, width)
    other = shift(chip, "c", 1)
    backs = jnp.stack(
        [
            jnp.dot(part, down_full, preferred_element_type=F32).reshape(NY, 2, own_rows, span)
            for part in (chip, other)
        ],
        0,
    )
    backward = backs[:, :, 0].reshape(rows, span)
    backward_tangent = backs[:, :, 1].reshape(rows, span)
    gate_tangent = (
        (backward_tangent * derivative + backward * curvature * tangent) * upward
    ).astype(BF16)

    every = jnp.concatenate(ring_gather(gate_tangent, "x"), 0)
    blocks = [
        lax.optimization_barrier(contract(turned[d], every, 1, 0).astype(BF16))
        for d in range(NZ)
    ]
    product = ring_sum(blocks, "z") / (rows * NX * NZ)

    entries = width * span * NY * NC
    scaled = product / 4096.0
    sums = jnp.concatenate(
        [
            jnp.sum(krylov * product[None], axis=(1, 2)),
            gram,
            jnp.sum(scaled * scaled).reshape(1),
        ]
    )
    sums = total(sums)
    projections = sums[:KRYLOV] / entries
    grams = sums[KRYLOV : KRYLOV + KRYLOV * KRYLOV].reshape(KRYLOV, KRYLOV) / entries
    mean_product = sums[-1] * (4096.0 * 4096.0 / entries)
    mean_square = (
        mean_product
        - 2.0 * jnp.sum(projections * projections)
        + jnp.sum(projections[:, None] * projections[None] * grams)
    )
    norm_value = jnp.sqrt(jnp.maximum(mean_square, 0.0) + epsilon)
    projected = product - jnp.sum(projections[:, None, None] * krylov, axis=0)
    next_vector = projected / norm_value
    coefficients = jnp.concatenate([projections, jnp.reshape(norm_value, (1,))])
    return (next_vector, coefficients)


def solution(mesh):
    split = Mesh(mesh.devices.reshape(NX, NZ, NY, NC), ("x", "z", "y", "c"))
    dp, mp = ("x", "z"), ("y", "c")
    placed = (
        P(dp, None),
        P(dp, None),
        P(dp, mp),
        P(dp, mp),
        P(dp, mp),
        P(None, dp, mp),
    )
    return jax.shard_map(
        local, mesh=split, in_specs=placed, out_specs=(P(dp, mp), P()), check_vma=False
    )
```

```python
import math

import jax
import jax.numpy as jnp
from jax import lax
from jax.experimental import pallas as pl
from jax.experimental.pallas import tpu as pltpu
from jax.sharding import Mesh
from jax.sharding import PartitionSpec as P

KRYLOV = 4
NX, NZ, NY, NC = 4, 8, 4, 2

root_scale = math.sqrt(2.0 / math.pi)
cubic_term = 0.044715
epsilon = 1e-06

F32 = jnp.float32
BF16 = jnp.bfloat16


def gelu_parts(values):
    inside = root_scale * (values + cubic_term * values * values * values)
    hyperbolic = jnp.tanh(inside)
    rising = root_scale * (1.0 + 3.0 * cubic_term * values * values)
    falloff = 1.0 - hyperbolic * hyperbolic
    result = 0.5 * values * (1.0 + hyperbolic)
    derivative = 0.5 * (1.0 + hyperbolic) + 0.5 * values * falloff * rising
    curvature = falloff * rising + 0.5 * values * falloff * (
        6.0 * root_scale * cubic_term * values - 2.0 * hyperbolic * rising * rising
    )
    return (result, derivative, curvature)


def contract(left, right, left_dim, right_dim):
    return lax.dot_general(
        left, right, (((left_dim,), (right_dim,)), ((), ())), preferred_element_type=F32
    )


def shift(value, axis, by):
    size = lax.axis_size(axis)
    return lax.ppermute(value, axis, [(i, (i + by) % size) for i in range(size)])


def rolled(value, dim, start):
    size = value.shape[dim]
    return lax.dynamic_slice_in_dim(jnp.concatenate([value, value], dim), start, size, dim)


def added(first, second):
    return (first.astype(F32) + second.astype(F32)).astype(BF16)


def added_front(whole, front):
    return lax.dynamic_update_slice_in_dim(whole, added(whole[: front.shape[0]], front), 0, 0)


def added_back(whole, back):
    rows = whole.shape[0] - back.shape[0]
    return lax.dynamic_update_slice_in_dim(whole, added(whole[rows:], back), rows, 0)


def ring_sum(blocks, axis):
    size = len(blocks)
    far = size // 2
    half = blocks[far].shape[0] // 2
    ahead = shift(blocks[far][:half], axis, 1)
    behind = shift(blocks[far][half:], axis, -1)
    onward = added_front(blocks[far - 1], ahead)
    backward = added_back(blocks[far + 1], behind)
    for step in range(far - 1, 0, -1):
        ahead = shift(onward, axis, 1)
        behind = shift(backward, axis, -1)
        if step > 1:
            onward = added(blocks[step - 1], ahead)
            backward = added(blocks[size - step + 1], behind)
    return blocks[0].astype(F32) + ahead.astype(F32) + behind.astype(F32)


def ring_gather(own, axis):
    far = lax.axis_size(axis) // 2
    half = own.shape[0] // 2
    before, after = [own], [own]
    for _ in range(1, far):
        before.append(shift(before[-1], axis, 1))
        after.append(shift(after[-1], axis, -1))
    farthest = jnp.concatenate(
        [shift(before[-1][:half], axis, 1), shift(after[-1][half:], axis, -1)], 0
    )
    return after + [farthest] + before[:0:-1]


def exchanged(value):
    devices = NX * NZ * NY * NC
    mine = jnp.zeros((128,), F32).at[: value.shape[0]].set(value)
    return lax.all_to_all(
        jnp.broadcast_to(mine, (devices, 128)), ("x", "z", "y", "c"), 0, 0, tiled=True
    )


VMEM = pl.BlockSpec(memory_space=pltpu.VMEM)
SMEM = pl.BlockSpec(memory_space=pltpu.SMEM)
LIMIT = pltpu.CompilerParams(vmem_limit_bytes=40 * 1024 * 1024)


def norm_kernel(place, tokens, own, *rest):
    sent, held = rest[: NX - 1], rest[NX - 1]
    count = held.shape[0]
    slab = own.shape[1]
    at_x, at_y, at_c = place[0], place[1], place[2]
    for c in range(NC):
        for y in range(NY):
            group = lax.rem(at_y + y, NY) * NC + lax.rem(at_c + c, NC)
            start = pl.multiple_of(group * count, count)
            values = tokens[pl.ds(start, count), :].astype(F32)
            square = jnp.mean(values * values, axis=1, keepdims=True)
            held[...] = (values * lax.rsqrt(square + epsilon)).astype(BF16)
            at = pl.ds((c * NY + y) * count, count)
            for ahead in range(NX if c == 0 else 1):
                columns = pl.ds(pl.multiple_of(lax.rem(at_x + ahead, NX) * slab, slab), slab)
                target = own if ahead == 0 else sent[ahead - 1]
                target[at, :] = held[:, columns]


def norm_tokens(place, tokens):
    rows, width = tokens.shape
    slab = width // NX
    shapes = [jax.ShapeDtypeStruct((rows, slab), BF16)]
    shapes += [jax.ShapeDtypeStruct((rows // NC, slab), BF16)] * (NX - 1)
    return pl.pallas_call(
        norm_kernel,
        out_shape=shapes,
        in_specs=[SMEM, VMEM],
        out_specs=[VMEM] * NX,
        scratch_shapes=[pltpu.VMEM((rows // (NC * NY), width), BF16)],
        compiler_params=LIMIT,
        cost_estimate=pl.CostEstimate(
            flops=4 * rows * width, bytes_accessed=4 * rows * width, transcendentals=rows
        ),
    )(place, tokens)


def forward_kernel(place, own, near, other, gathered, *rest):
    parts, (around, terms, matrix) = rest[: NZ + 1], rest[NZ + 1 :]
    depth = parts[0].shape[0]
    half = near.shape[1]
    two = gathered.shape[1]
    at = 0
    for part in parts:
        count = part.shape[0]
        ahead, offset = at // depth, at % depth
        start = lax.rem(place[3] + ahead, NZ) * depth + offset
        matrix[pl.ds(pl.multiple_of(start, count), count), :] = part[...]
        at += count
    around[0] = own[...]
    for d in range(1, NX):
        around[d, :half, :] = near[d - 1]
        around[d, half:, :] = other[d - 1]
    for d in range(NX):
        terms[d, :, :two] = jnp.dot(
            around[d], gathered[...], preferred_element_type=F32
        ).astype(BF16)
        terms[d, :, two:] = jnp.dot(
            around[d], matrix[...], preferred_element_type=F32
        ).astype(BF16)


def forward_terms(place, own, near, other, gathered, parts):
    rows, slab = own.shape
    span = parts[0].shape[1]
    width = gathered.shape[1] + span
    return pl.pallas_call(
        forward_kernel,
        out_shape=[
            jax.ShapeDtypeStruct((NX, rows, slab), BF16),
            jax.ShapeDtypeStruct((NX, rows, width), BF16),
        ],
        in_specs=[SMEM] + [VMEM] * (4 + len(parts)),
        out_specs=[VMEM] * 2,
        scratch_shapes=[pltpu.VMEM((slab, span), BF16)],
        compiler_params=LIMIT,
        cost_estimate=pl.CostEstimate(
            flops=2 * NX * rows * slab * width,
            bytes_accessed=2 * (2 * NX * rows * slab + slab * width + NX * rows * width),
            transcendentals=0,
        ),
    )(place, own, near, other, gathered, *parts)


def end_kernel(entries, every, product, krylov, vector, coefficients):
    sums = jnp.sum(every[...], axis=0, keepdims=True)
    lane = lax.broadcasted_iota(jnp.int32, sums.shape, 1)

    def at(place):
        return jnp.sum(jnp.where(lane == place, sums, 0.0), axis=1, keepdims=True)

    projections = [at(i) / entries for i in range(KRYLOV)]
    mean_square = at(KRYLOV + KRYLOV * KRYLOV) * (4096.0 * 4096.0 / entries)
    for i in range(KRYLOV):
        mean_square -= 2.0 * projections[i] * projections[i]
    for i in range(KRYLOV):
        for j in range(KRYLOV):
            gram = at(KRYLOV + KRYLOV * i + j) / entries
            mean_square += projections[i] * projections[j] * gram
    norm_value = jnp.sqrt(jnp.maximum(mean_square, 0.0) + epsilon)
    row = jnp.where(lane == KRYLOV, norm_value, 0.0)
    projected = product[...]
    for i in range(KRYLOV):
        projected -= projections[i] * krylov[i]
        row = jnp.where(lane == i, projections[i], row)
    vector[...] = projected / norm_value
    coefficients[...] = row


def finish(entries, every, product, krylov):
    return pl.pallas_call(
        lambda *refs: end_kernel(entries, *refs),
        out_shape=[
            jax.ShapeDtypeStruct(product.shape, F32),
            jax.ShapeDtypeStruct((1, every.shape[1]), F32),
        ],
        in_specs=[VMEM] * 3,
        out_specs=[VMEM] * 2,
        compiler_params=LIMIT,
        cost_estimate=pl.CostEstimate(
            flops=10 * product.size, bytes_accessed=24 * product.size, transcendentals=1
        ),
    )(every, product, krylov)


def local(tokens, targets, gate_weight, up_weight, down_weight, krylov):
    rows, width = tokens.shape
    depth, span = gate_weight.shape
    own_rows = rows // (NY * NC)
    slab = width // NX
    at_x, at_z, at_y, at_c = (lax.axis_index(name) for name in ("x", "z", "y", "c"))

    gathered = lax.all_gather(
        jnp.concatenate([gate_weight, up_weight], 1), "z", axis=0, tiled=True
    )
    direction = krylov[KRYLOV - 1].astype(BF16)
    before, after = [direction], [direction]
    before.append(shift(direction, "z", 1))
    after.append(shift(direction, "z", -1))
    down_before, down_after = shift(down_weight, "x", 1), shift(down_weight, "x", -1)

    place = jnp.stack([at_x, at_y, at_c, at_z]).astype(jnp.int32)
    own, *sent = norm_tokens(place, tokens)
    before[1], after[1], down_before, down_after, own, sent = lax.optimization_barrier(
        (before[1], after[1], down_before, down_after, own, sent)
    )
    near = [shift(sent[ahead - 1], "x", ahead) for ahead in range(NX - 1, 0, -1)]
    before.append(shift(before[1], "z", 1))
    after.append(shift(after[1], "z", -1))
    middle = depth // 2
    down_far = [shift(down_before[:middle], "x", 1), shift(down_after[middle:], "x", -1)]
    before[2], after[2], near, down_far = lax.optimization_barrier(
        (before[2], after[2], near, down_far)
    )

    across = jnp.concatenate([down_weight, down_after, *down_far, down_before], 0)
    down_full = lax.all_gather(across, "z", axis=0, tiled=True)

    before.append(shift(before[2], "z", 1))
    after.append(shift(after[2], "z", -1))
    near = jnp.stack(near, 0)
    other = shift(near, "c", 1)
    far = [shift(before[3][:middle], "z", 1), shift(after[3][middle:], "z", -1)]
    parts = after + far + before[:0:-1]
    around, terms = forward_terms(place, own, near, other, gathered, parts)

    def arranged(values):
        values = rolled(values.reshape(own_rows, NX, NZ, depth), 1, at_x)
        return jnp.swapaxes(values, 1, 2).reshape(own_rows, width)

    start = (at_y * NC + at_c) * own_rows
    own_tokens, own_targets = (
        arranged(lax.dynamic_slice_in_dim(a, start, own_rows, 0)) for a in (tokens, targets)
    )
    turned = rolled(around.reshape(NX * rows, slab).T.reshape(NZ, depth, NX * rows), 0, at_z)
    gram = jnp.sum(krylov[:, None] * krylov[None], axis=(2, 3)).reshape(-1)
    forward = ring_sum([terms[d] for d in range(NX)], "x")
    gate, upward, tangent = jnp.split(forward, 3, axis=1)
    activated, derivative, curvature = gelu_parts(gate)
    hidden = (activated * upward).astype(BF16)
    hidden_tangent = (derivative * tangent * upward).astype(BF16)
    both = jnp.stack(
        [a.reshape(NC, NY, own_rows, span) for a in (hidden, hidden_tangent)], 2
    ).reshape(NC, NY * 2 * own_rows, span)

    both, down_full, turned, gram, own_tokens, own_targets = lax.optimization_barrier(
        (both, down_full, turned, gram, own_tokens, own_targets)
    )

    theirs = shift(contract(both[1], down_full, 1, 1).astype(BF16), "c", 1)
    mine = lax.optimization_barrier(contract(both[0], down_full, 1, 1).astype(BF16))
    mine, theirs = (a.reshape(NY, 2, own_rows, width) for a in (mine, theirs))
    mine = lax.optimization_barrier([added(mine[d], theirs[d]) for d in range(NY)])
    outputs, outputs_tangent = ring_sum(mine, "y")
    residual = (own_tokens.astype(F32) + outputs - own_targets.astype(F32)).astype(BF16)
    residuals = jnp.stack([residual, outputs_tangent.astype(BF16)], 0)
    chip = jnp.stack(ring_gather(residuals, "y"), 0).reshape(NY * 2 * own_rows, width)
    other = shift(chip, "c", 1)
    backs = jnp.stack(
        [
            jnp.dot(part, down_full, preferred_element_type=F32).reshape(NY, 2, own_rows, span)
            for part in (chip, other)
        ],
        0,
    )
    backward = backs[:, :, 0].reshape(rows, span)
    backward_tangent = backs[:, :, 1].reshape(rows, span)
    gate_tangent = (
        (backward_tangent * derivative + backward * curvature * tangent) * upward
    ).astype(BF16)

    every = jnp.concatenate(ring_gather(gate_tangent, "x"), 0)
    blocks = [
        lax.optimization_barrier(contract(turned[d], every, 1, 0).astype(BF16))
        for d in range(NZ)
    ]
    product = ring_sum(blocks, "z") / (rows * NX * NZ)

    entries = width * span * NY * NC
    scaled = product / 4096.0
    sums = jnp.concatenate(
        [
            jnp.sum(krylov * product[None], axis=(1, 2)),
            gram,
            jnp.sum(scaled * scaled).reshape(1),
        ]
    )
    next_vector, row = finish(float(entries), exchanged(sums), product, krylov)
    return (next_vector, row[0, : KRYLOV + 1])


def solution(mesh):
    split = Mesh(mesh.devices.reshape(NX, NZ, NY, NC), ("x", "z", "y", "c"))
    dp, mp = ("x", "z"), ("y", "c")
    placed = (
        P(dp, None),
        P(dp, None),
        P(dp, mp),
        P(dp, mp),
        P(dp, mp),
        P(None, dp, mp),
    )
    return jax.shard_map(
        local, mesh=split, in_specs=placed, out_specs=(P(dp, mp), P()), check_vma=False
    )
```

```python
import math

import jax
import jax.numpy as jnp
from jax import lax
from jax.experimental import pallas as pl
from jax.experimental.pallas import tpu as pltpu
from jax.sharding import Mesh
from jax.sharding import PartitionSpec as P

KRYLOV = 4
NX, NZ, NY, NC = 4, 8, 4, 2

root_scale = math.sqrt(2.0 / math.pi)
cubic_term = 0.044715
epsilon = 1e-06

F32 = jnp.float32
BF16 = jnp.bfloat16


def gelu_parts(values):
    inside = root_scale * (values + cubic_term * values * values * values)
    hyperbolic = jnp.tanh(inside)
    rising = root_scale * (1.0 + 3.0 * cubic_term * values * values)
    falloff = 1.0 - hyperbolic * hyperbolic
    result = 0.5 * values * (1.0 + hyperbolic)
    derivative = 0.5 * (1.0 + hyperbolic) + 0.5 * values * falloff * rising
    curvature = falloff * rising + 0.5 * values * falloff * (
        6.0 * root_scale * cubic_term * values - 2.0 * hyperbolic * rising * rising
    )
    return (result, derivative, curvature)


def contract(left, right, left_dim, right_dim):
    return lax.dot_general(
        left, right, (((left_dim,), (right_dim,)), ((), ())), preferred_element_type=F32
    )


def shift(value, axis, by):
    size = lax.axis_size(axis)
    return lax.ppermute(value, axis, [(i, (i + by) % size) for i in range(size)])


def rolled(value, dim, start):
    size = value.shape[dim]
    return lax.dynamic_slice_in_dim(jnp.concatenate([value, value], dim), start, size, dim)


def added(first, second):
    return (first.astype(F32) + second.astype(F32)).astype(BF16)


def added_front(whole, front):
    return lax.dynamic_update_slice_in_dim(whole, added(whole[: front.shape[0]], front), 0, 0)


def added_back(whole, back):
    rows = whole.shape[0] - back.shape[0]
    return lax.dynamic_update_slice_in_dim(whole, added(whole[rows:], back), rows, 0)


def both_ways(onward, backward, axis):
    onward, backward = lax.optimization_barrier((onward, backward))
    return shift(onward, axis, 1), shift(backward, axis, -1)


def ring_sum(blocks, axis):
    size = len(blocks)
    far = size // 2
    ahead, behind = both_ways(*blocks[far], axis)
    onward = added_front(blocks[far - 1], ahead)
    backward = added_back(blocks[far + 1], behind)
    for step in range(far - 1, 0, -1):
        ahead, behind = both_ways(onward, backward, axis)
        if step > 1:
            onward = added(blocks[step - 1], ahead)
            backward = added(blocks[size - step + 1], behind)
    return blocks[0].astype(F32) + ahead.astype(F32) + behind.astype(F32)


def ring_gather(own, axis):
    far = lax.axis_size(axis) // 2
    half = own.shape[0] // 2
    before, after = [own], [own]
    for _ in range(1, far):
        ahead, behind = both_ways(before[-1], after[-1], axis)
        before.append(ahead)
        after.append(behind)
    farthest = both_ways(before[-1][:half], after[-1][half:], axis)
    return after + [*farthest] + before[:0:-1]


def exchanged(value):
    devices = NX * NZ * NY * NC
    mine = jnp.zeros((128,), F32).at[: value.shape[0]].set(value)
    return lax.all_to_all(
        jnp.broadcast_to(mine, (devices, 128)), ("x", "z", "y", "c"), 0, 0, tiled=True
    )


VMEM = pl.BlockSpec(memory_space=pltpu.VMEM)
SMEM = pl.BlockSpec(memory_space=pltpu.SMEM)
LIMIT = pltpu.CompilerParams(vmem_limit_bytes=40 * 1024 * 1024)


def norm_kernel(place, tokens, own, *rest):
    sent, held = rest[: NX - 1], rest[NX - 1]
    count = held.shape[0]
    slab = own.shape[1]
    at_x, at_y, at_c = place[0], place[1], place[2]
    for c in range(NC):
        for y in range(NY):
            group = lax.rem(at_y + y, NY) * NC + lax.rem(at_c + c, NC)
            start = pl.multiple_of(group * count, count)
            values = tokens[pl.ds(start, count), :].astype(F32)
            square = jnp.mean(values * values, axis=1, keepdims=True)
            held[...] = (values * lax.rsqrt(square + epsilon)).astype(BF16)
            at = pl.ds((c * NY + y) * count, count)
            for ahead in range(NX if c == 0 else 1):
                columns = pl.ds(pl.multiple_of(lax.rem(at_x + ahead, NX) * slab, slab), slab)
                target = own if ahead == 0 else sent[ahead - 1]
                target[at, :] = held[:, columns]


def norm_tokens(place, tokens):
    rows, width = tokens.shape
    slab = width // NX
    shapes = [jax.ShapeDtypeStruct((rows, slab), BF16)]
    shapes += [jax.ShapeDtypeStruct((rows // NC, slab), BF16)] * (NX - 1)
    return pl.pallas_call(
        norm_kernel,
        out_shape=shapes,
        in_specs=[SMEM, VMEM],
        out_specs=[VMEM] * NX,
        scratch_shapes=[pltpu.VMEM((rows // (NC * NY), width), BF16)],
        compiler_params=LIMIT,
        cost_estimate=pl.CostEstimate(
            flops=4 * rows * width, bytes_accessed=4 * rows * width, transcendentals=rows
        ),
    )(place, tokens)


def forward_kernel(place, own, near, other, gathered, *rest):
    parts, (around, *terms), matrix = rest[: NZ + 1], rest[NZ + 1 : -1], rest[-1]
    depth = parts[0].shape[0]
    half = near.shape[1]
    two = gathered.shape[1]
    at = 0
    for part in parts:
        count = part.shape[0]
        ahead, offset = at // depth, at % depth
        start = lax.rem(place[3] + ahead, NZ) * depth + offset
        matrix[pl.ds(pl.multiple_of(start, count), count), :] = part[...]
        at += count
    around[0] = own[...]
    for d in range(1, NX):
        around[d, :half, :] = near[d - 1]
        around[d, half:, :] = other[d - 1]
    ours, after, low, high, before = terms
    for d, targets in enumerate(((ours,), (after,), (low, high), (before,))):
        for matrix_of, columns in ((gathered, slice(0, two)), (matrix, slice(two, None))):
            values = jnp.dot(around[d], matrix_of[...], preferred_element_type=F32).astype(BF16)
            at = 0
            for target in targets:
                target[:, columns] = values[at : at + target.shape[0]]
                at += target.shape[0]


def forward_terms(place, own, near, other, gathered, parts):
    rows, slab = own.shape
    span = parts[0].shape[1]
    width = gathered.shape[1] + span
    return pl.pallas_call(
        forward_kernel,
        out_shape=[
            jax.ShapeDtypeStruct((NX, rows, slab), BF16),
            *(
                jax.ShapeDtypeStruct((count, width), BF16)
                for count in (rows, rows, rows // 2, rows // 2, rows)
            ),
        ],
        in_specs=[SMEM] + [VMEM] * (4 + len(parts)),
        out_specs=[VMEM] * 6,
        scratch_shapes=[pltpu.VMEM((slab, span), BF16)],
        compiler_params=LIMIT,
        cost_estimate=pl.CostEstimate(
            flops=2 * NX * rows * slab * width,
            bytes_accessed=2 * (2 * NX * rows * slab + slab * width + NX * rows * width),
            transcendentals=0,
        ),
    )(place, own, near, other, gathered, *parts)


def product_kernel(turned, *rest):
    parts, targets, every = rest[: NX + 1], rest[NX + 1 : -1], rest[-1]
    at = 0
    for part in parts:
        every[at : at + part.shape[0], :] = part[...]
        at += part.shape[0]
    depth = turned.shape[1]
    for pair in range(0, NZ, 2):
        rows = turned[pair : pair + 2].reshape(2 * depth, every.shape[0])
        values = jnp.dot(rows, every[...], preferred_element_type=F32).astype(BF16)
        if pair == NZ // 2:
            pieces = [targets[pair], targets[pair + 1], targets[pair + 2]]
        else:
            pieces = targets[pair + (pair > NZ // 2) :][:2]
        at = 0
        for target in pieces:
            target[...] = values[at : at + target.shape[0]]
            at += target.shape[0]


def product_terms(turned, parts):
    depth, span = turned.shape[1], parts[0].shape[1]
    counts = [depth] * NZ
    counts[NZ // 2 : NZ // 2 + 1] = [depth // 2] * 2
    return pl.pallas_call(
        product_kernel,
        out_shape=[jax.ShapeDtypeStruct((count, span), BF16) for count in counts],
        in_specs=[VMEM] * (1 + len(parts)),
        out_specs=[VMEM] * len(counts),
        scratch_shapes=[pltpu.VMEM((turned.shape[2], span), BF16)],
        compiler_params=LIMIT,
        cost_estimate=pl.CostEstimate(
            flops=2 * turned.size * span,
            bytes_accessed=2 * (turned.size + (turned.shape[2] + NZ * depth) * span),
            transcendentals=0,
        ),
    )(turned, *parts)


def end_kernel(entries, every, product, krylov, vector, coefficients):
    sums = jnp.sum(every[...], axis=0, keepdims=True)
    lane = lax.broadcasted_iota(jnp.int32, sums.shape, 1)

    def at(place):
        return jnp.sum(jnp.where(lane == place, sums, 0.0), axis=1, keepdims=True)

    projections = [at(i) / entries for i in range(KRYLOV)]
    mean_square = at(KRYLOV + KRYLOV * KRYLOV) * (4096.0 * 4096.0 / entries)
    for i in range(KRYLOV):
        mean_square -= 2.0 * projections[i] * projections[i]
    for i in range(KRYLOV):
        for j in range(KRYLOV):
            gram = at(KRYLOV + KRYLOV * i + j) / entries
            mean_square += projections[i] * projections[j] * gram
    norm_value = jnp.sqrt(jnp.maximum(mean_square, 0.0) + epsilon)
    row = jnp.where(lane == KRYLOV, norm_value, 0.0)
    projected = product[...]
    for i in range(KRYLOV):
        projected -= projections[i] * krylov[i]
        row = jnp.where(lane == i, projections[i], row)
    vector[...] = projected / norm_value
    coefficients[...] = row


def finish(entries, every, product, krylov):
    return pl.pallas_call(
        lambda *refs: end_kernel(entries, *refs),
        out_shape=[
            jax.ShapeDtypeStruct(product.shape, F32),
            jax.ShapeDtypeStruct((1, every.shape[1]), F32),
        ],
        in_specs=[VMEM] * 3,
        out_specs=[VMEM] * 2,
        compiler_params=LIMIT,
        cost_estimate=pl.CostEstimate(
            flops=10 * product.size, bytes_accessed=24 * product.size, transcendentals=1
        ),
    )(every, product, krylov)


def local(tokens, targets, gate_weight, up_weight, down_weight, krylov):
    rows, width = tokens.shape
    depth, span = gate_weight.shape
    own_rows = rows // (NY * NC)
    slab = width // NX
    at_x, at_z, at_y, at_c = (lax.axis_index(name) for name in ("x", "z", "y", "c"))

    gathered = lax.all_gather(
        jnp.concatenate([gate_weight, up_weight], 1), "z", axis=0, tiled=True
    )
    direction = krylov[KRYLOV - 1].astype(BF16)
    before, after = [direction], [direction]
    before.append(shift(direction, "z", 1))
    after.append(shift(direction, "z", -1))
    down_before, down_after = shift(down_weight, "x", 1), shift(down_weight, "x", -1)

    place = jnp.stack([at_x, at_y, at_c, at_z]).astype(jnp.int32)
    own, *sent = norm_tokens(place, tokens)
    before[1], after[1], down_before, down_after, own, sent = lax.optimization_barrier(
        (before[1], after[1], down_before, down_after, own, sent)
    )
    near = [shift(sent[ahead - 1], "x", ahead) for ahead in range(NX - 1, 0, -1)]
    before.append(shift(before[1], "z", 1))
    after.append(shift(after[1], "z", -1))
    middle = depth // 2
    down_far = [shift(down_before[:middle], "x", 1), shift(down_after[middle:], "x", -1)]
    before[2], after[2], near, down_far = lax.optimization_barrier(
        (before[2], after[2], near, down_far)
    )

    across = jnp.concatenate([down_weight, down_after, *down_far, down_before], 0)
    down_full = lax.all_gather(across, "z", axis=0, tiled=True)

    before.append(shift(before[2], "z", 1))
    after.append(shift(after[2], "z", -1))
    near = jnp.stack(near, 0)
    other = shift(near, "c", 1)
    far = [shift(before[3][:middle], "z", 1), shift(after[3][middle:], "z", -1)]
    parts = after + far + before[:0:-1]
    around, ours, ours_after, low, high, ours_before = forward_terms(place, own, near, other, gathered, parts)

    def arranged(values):
        values = rolled(values.reshape(own_rows, NX, NZ, depth), 1, at_x)
        return jnp.swapaxes(values, 1, 2).reshape(own_rows, width)

    start = (at_y * NC + at_c) * own_rows
    own_tokens, own_targets = (
        arranged(lax.dynamic_slice_in_dim(a, start, own_rows, 0)) for a in (tokens, targets)
    )
    turned = rolled(around.reshape(NX * rows, slab).T.reshape(NZ, depth, NX * rows), 0, at_z)
    gram = jnp.sum(krylov[:, None] * krylov[None], axis=(2, 3)).reshape(-1)
    forward = ring_sum([ours, ours_after, (low, high), ours_before], "x")
    gate, upward, tangent = jnp.split(forward, 3, axis=1)
    activated, derivative, curvature = gelu_parts(gate)
    hidden = (activated * upward).astype(BF16)
    hidden_tangent = (derivative * tangent * upward).astype(BF16)
    both = jnp.stack(
        [a.reshape(NC, NY, own_rows, span) for a in (hidden, hidden_tangent)], 2
    ).reshape(NC, NY * 2 * own_rows, span)

    both, down_full, turned, gram, own_tokens, own_targets = lax.optimization_barrier(
        (both, down_full, turned, gram, own_tokens, own_targets)
    )

    theirs = shift(contract(both[1], down_full, 1, 1).astype(BF16), "c", 1)
    mine = lax.optimization_barrier(contract(both[0], down_full, 1, 1).astype(BF16))
    mine, theirs = (a.reshape(NY, 2, own_rows, width) for a in (mine, theirs))
    mine = [added(mine[d], theirs[d]) for d in range(NY)]
    mine[2] = (mine[2][:1], mine[2][1:])
    outputs, outputs_tangent = ring_sum(lax.optimization_barrier(mine), "y")
    residual = (own_tokens.astype(F32) + outputs - own_targets.astype(F32)).astype(BF16)
    residuals = jnp.stack([residual, outputs_tangent.astype(BF16)], 0)
    chip = jnp.concatenate(ring_gather(residuals, "y"), 0).reshape(NY * 2 * own_rows, width)
    other = shift(chip, "c", 1)
    backs = jnp.stack(
        [
            jnp.dot(part, down_full, preferred_element_type=F32).reshape(NY, 2, own_rows, span)
            for part in (chip, other)
        ],
        0,
    )
    backward = backs[:, :, 0].reshape(rows, span)
    backward_tangent = backs[:, :, 1].reshape(rows, span)
    gate_tangent = (
        (backward_tangent * derivative + backward * curvature * tangent) * upward
    ).astype(BF16)

    blocks = list(product_terms(turned, ring_gather(gate_tangent, "x")))
    blocks[NZ // 2 : NZ // 2 + 2] = [tuple(blocks[NZ // 2 : NZ // 2 + 2])]
    product = ring_sum(blocks, "z") / (rows * NX * NZ)

    entries = width * span * NY * NC
    scaled = product / 4096.0
    sums = jnp.concatenate(
        [
            jnp.sum(krylov * product[None], axis=(1, 2)),
            gram,
            jnp.sum(scaled * scaled).reshape(1),
        ]
    )
    next_vector, row = finish(float(entries), exchanged(sums), product, krylov)
    return (next_vector, row[0, : KRYLOV + 1])


def solution(mesh):
    split = Mesh(mesh.devices.reshape(NX, NZ, NY, NC), ("x", "z", "y", "c"))
    dp, mp = ("x", "z"), ("y", "c")
    placed = (
        P(dp, None),
        P(dp, None),
        P(dp, mp),
        P(dp, mp),
        P(dp, mp),
        P(None, dp, mp),
    )
    return jax.shard_map(
        local, mesh=split, in_specs=placed, out_specs=(P(dp, mp), P()), check_vma=False
    )
```

```python
import math

import jax
import jax.numpy as jnp
from jax import lax
from jax.experimental import pallas as pl
from jax.experimental.pallas import tpu as pltpu
from jax.sharding import Mesh
from jax.sharding import PartitionSpec as P

KRYLOV = 4
NX, NZ, NY, NC = 4, 8, 4, 2

root_scale = math.sqrt(2.0 / math.pi)
cubic_term = 0.044715
epsilon = 1e-06

F32 = jnp.float32
BF16 = jnp.bfloat16


def gelu_parts(values):
    inside = root_scale * (values + cubic_term * values * values * values)
    hyperbolic = jnp.tanh(inside)
    rising = root_scale * (1.0 + 3.0 * cubic_term * values * values)
    falloff = 1.0 - hyperbolic * hyperbolic
    result = 0.5 * values * (1.0 + hyperbolic)
    derivative = 0.5 * (1.0 + hyperbolic) + 0.5 * values * falloff * rising
    curvature = falloff * rising + 0.5 * values * falloff * (
        6.0 * root_scale * cubic_term * values - 2.0 * hyperbolic * rising * rising
    )
    return (result, derivative, curvature)


def contract(left, right, left_dim, right_dim):
    return lax.dot_general(
        left, right, (((left_dim,), (right_dim,)), ((), ())), preferred_element_type=F32
    )


def shift(value, axis, by):
    size = lax.axis_size(axis)
    return lax.ppermute(value, axis, [(i, (i + by) % size) for i in range(size)])


def rolled(value, dim, start):
    size = value.shape[dim]
    return lax.dynamic_slice_in_dim(jnp.concatenate([value, value], dim), start, size, dim)


def added(first, second):
    return (first.astype(F32) + second.astype(F32)).astype(BF16)


def added_front(whole, front):
    return lax.dynamic_update_slice_in_dim(whole, added(whole[: front.shape[0]], front), 0, 0)


def added_back(whole, back):
    rows = whole.shape[0] - back.shape[0]
    return lax.dynamic_update_slice_in_dim(whole, added(whole[rows:], back), rows, 0)


def ring_sum(blocks, axis):
    size = len(blocks)
    far = size // 2
    half = blocks[far].shape[0] // 2
    ahead = shift(blocks[far][:half], axis, 1)
    behind = shift(blocks[far][half:], axis, -1)
    onward = added_front(blocks[far - 1], ahead)
    backward = added_back(blocks[far + 1], behind)
    for step in range(far - 1, 0, -1):
        ahead = shift(onward, axis, 1)
        behind = shift(backward, axis, -1)
        if step > 1:
            onward = added(blocks[step - 1], ahead)
            backward = added(blocks[size - step + 1], behind)
    return blocks[0].astype(F32) + ahead.astype(F32) + behind.astype(F32)


def ring_gather(own, axis):
    far = lax.axis_size(axis) // 2
    half = own.shape[0] // 2
    before, after = [own], [own]
    for _ in range(1, far):
        before.append(shift(before[-1], axis, 1))
        after.append(shift(after[-1], axis, -1))
    farthest = jnp.concatenate(
        [shift(before[-1][:half], axis, 1), shift(after[-1][half:], axis, -1)], 0
    )
    return after + [farthest] + before[:0:-1]


def exchanged(value):
    devices = NX * NZ * NY * NC
    mine = jnp.zeros((128,), F32).at[: value.shape[0]].set(value)
    return lax.all_to_all(
        jnp.broadcast_to(mine, (devices, 128)), ("x", "z", "y", "c"), 0, 0, tiled=True
    )


VMEM = pl.BlockSpec(memory_space=pltpu.VMEM)
SMEM = pl.BlockSpec(memory_space=pltpu.SMEM)
LIMIT = pltpu.CompilerParams(vmem_limit_bytes=40 * 1024 * 1024)


def norm_kernel(place, tokens, own, *rest):
    sent, held = rest[: NX - 1], rest[NX - 1]
    count = held.shape[0]
    slab = own.shape[1]
    at_x, at_y, at_c = place[0], place[1], place[2]
    for c in range(NC):
        for y in range(NY):
            group = lax.rem(at_y + y, NY) * NC + lax.rem(at_c + c, NC)
            start = pl.multiple_of(group * count, count)
            values = tokens[pl.ds(start, count), :].astype(F32)
            square = jnp.mean(values * values, axis=1, keepdims=True)
            held[...] = (values * lax.rsqrt(square + epsilon)).astype(BF16)
            at = pl.ds((c * NY + y) * count, count)
            for ahead in range(NX if c == 0 else 1):
                columns = pl.ds(pl.multiple_of(lax.rem(at_x + ahead, NX) * slab, slab), slab)
                target = own if ahead == 0 else sent[ahead - 1]
                target[at, :] = held[:, columns]


def norm_tokens(place, tokens):
    rows, width = tokens.shape
    slab = width // NX
    shapes = [jax.ShapeDtypeStruct((rows, slab), BF16)]
    shapes += [jax.ShapeDtypeStruct((rows // NC, slab), BF16)] * (NX - 1)
    return pl.pallas_call(
        norm_kernel,
        out_shape=shapes,
        in_specs=[SMEM, VMEM],
        out_specs=[VMEM] * NX,
        scratch_shapes=[pltpu.VMEM((rows // (NC * NY), width), BF16)],
        compiler_params=LIMIT,
        cost_estimate=pl.CostEstimate(
            flops=4 * rows * width, bytes_accessed=4 * rows * width, transcendentals=rows
        ),
    )(place, tokens)


def forward_kernel(place, own, near, other, gathered, *rest):
    parts, (around, terms, matrix, pair, arrived) = rest[: NZ + 1], rest[NZ + 1 :]
    depth = parts[0].shape[0]
    half = near.shape[1]
    two = pair.shape[1]
    moves = [(own, around.at[0]), (gathered.at[:, :two], pair)]
    for d in range(1, NX):
        moves.append((near.at[d - 1], around.at[d, :half]))
        moves.append((other.at[d - 1], around.at[d, half:]))
    at = 0
    for part in parts:
        count = part.shape[0]
        ahead, offset = at // depth, at % depth
        start = lax.rem(place[3] + ahead, NZ) * depth + offset
        moves.append((part, matrix.at[pl.ds(pl.multiple_of(start, count), count)]))
        at += count
    copies = [
        pltpu.make_async_copy(source, target, arrived.at[i])
        for i, (source, target) in enumerate(moves)
    ]
    for copy in copies:
        copy.start()
    for copy in copies:
        copy.wait()
    for d in range(NX):
        terms[d, :, :two] = jnp.dot(around[d], pair[...], preferred_element_type=F32).astype(BF16)
        terms[d, :, two:] = jnp.dot(
            around[d], matrix[...], preferred_element_type=F32
        ).astype(BF16)


def forward_terms(place, own, near, other, gathered, parts):
    rows, slab = own.shape
    span = parts[0].shape[1]
    width = 3 * span
    anywhere = pl.BlockSpec(memory_space=pl.ANY)
    return pl.pallas_call(
        forward_kernel,
        out_shape=[
            jax.ShapeDtypeStruct((NX, rows, slab), BF16),
            jax.ShapeDtypeStruct((NX, rows, width), BF16),
        ],
        in_specs=[SMEM] + [anywhere] * (4 + len(parts)),
        out_specs=[VMEM] * 2,
        scratch_shapes=[
            pltpu.VMEM((slab, span), BF16),
            pltpu.VMEM((slab, 2 * span), BF16),
            pltpu.SemaphoreType.DMA((2 + 2 * (NX - 1) + len(parts),)),
        ],
        compiler_params=LIMIT,
        cost_estimate=pl.CostEstimate(
            flops=2 * NX * rows * slab * width,
            bytes_accessed=2 * (2 * NX * rows * slab + slab * width + NX * rows * width),
            transcendentals=0,
        ),
    )(place, own, near, other, gathered, *parts)


def partial_kernel(units, most, others, partial):
    cut = most.shape[1]
    dims = (((1,), (1,)), ((), ()))
    values = lax.dot_general(units[:, :cut], most[...], dims, preferred_element_type=F32)
    values += lax.dot_general(units[:, cut:], others[...], dims, preferred_element_type=F32)
    partial[...] = values.astype(BF16)


def partial_outputs(units, most, others):
    rows, span = units.shape
    width, cut = most.shape
    slab = width // NX
    return pl.pallas_call(
        partial_kernel,
        grid=(NX,),
        out_shape=jax.ShapeDtypeStruct((rows, width), BF16),
        in_specs=[
            pl.BlockSpec((rows, span), lambda i: (0, 0)),
            pl.BlockSpec((slab, cut), lambda i: (i, 0)),
            pl.BlockSpec((slab, span - cut), lambda i: (i, 0)),
        ],
        out_specs=pl.BlockSpec((rows, slab), lambda i: (0, i)),
        compiler_params=LIMIT,
        cost_estimate=pl.CostEstimate(
            flops=2 * rows * span * width,
            bytes_accessed=2 * (rows * span + width * span + rows * width),
            transcendentals=0,
        ),
    )(units, most, others)


def end_kernel(entries, every, product, krylov, vector, coefficients):
    sums = jnp.sum(every[...], axis=0, keepdims=True)
    lane = lax.broadcasted_iota(jnp.int32, sums.shape, 1)

    def at(place):
        return jnp.sum(jnp.where(lane == place, sums, 0.0), axis=1, keepdims=True)

    projections = [at(i) / entries for i in range(KRYLOV)]
    mean_square = at(KRYLOV + KRYLOV * KRYLOV) * (4096.0 * 4096.0 / entries)
    for i in range(KRYLOV):
        mean_square -= 2.0 * projections[i] * projections[i]
    for i in range(KRYLOV):
        for j in range(KRYLOV):
            gram = at(KRYLOV + KRYLOV * i + j) / entries
            mean_square += projections[i] * projections[j] * gram
    norm_value = jnp.sqrt(jnp.maximum(mean_square, 0.0) + epsilon)
    row = jnp.where(lane == KRYLOV, norm_value, 0.0)
    projected = product[...]
    for i in range(KRYLOV):
        projected -= projections[i] * krylov[i]
        row = jnp.where(lane == i, projections[i], row)
    vector[...] = projected / norm_value
    coefficients[...] = row


def finish(entries, every, product, krylov):
    return pl.pallas_call(
        lambda *refs: end_kernel(entries, *refs),
        out_shape=[
            jax.ShapeDtypeStruct(product.shape, F32),
            jax.ShapeDtypeStruct((1, every.shape[1]), F32),
        ],
        in_specs=[VMEM] * 3,
        out_specs=[VMEM] * 2,
        compiler_params=LIMIT,
        cost_estimate=pl.CostEstimate(
            flops=10 * product.size, bytes_accessed=24 * product.size, transcendentals=1
        ),
    )(every, product, krylov)


def local(tokens, targets, gate_weight, up_weight, down_weight, krylov):
    rows, width = tokens.shape
    depth, span = gate_weight.shape
    own_rows = rows // (NY * NC)
    slab = width // NX
    at_x, at_z, at_y, at_c = (lax.axis_index(name) for name in ("x", "z", "y", "c"))

    cut = span * 4 // 5
    gathered = lax.all_gather(
        jnp.concatenate([gate_weight, up_weight, down_weight[:, cut:]], 1),
        "z",
        axis=0,
        tiled=True,
    )
    down_weight = down_weight[:, :cut]
    direction = krylov[KRYLOV - 1].astype(BF16)
    before, after = [direction], [direction]
    before.append(shift(direction, "z", 1))
    after.append(shift(direction, "z", -1))
    down_before, down_after = shift(down_weight, "x", 1), shift(down_weight, "x", -1)

    place = jnp.stack([at_x, at_y, at_c, at_z]).astype(jnp.int32)
    own, *sent = norm_tokens(place, tokens)
    before[1], after[1], down_before, down_after, own, sent = lax.optimization_barrier(
        (before[1], after[1], down_before, down_after, own, sent)
    )
    near = [shift(sent[ahead - 1], "x", ahead) for ahead in range(NX - 1, 0, -1)]
    before.append(shift(before[1], "z", 1))
    after.append(shift(after[1], "z", -1))
    middle = depth // 2
    down_far = [shift(down_before[:middle], "x", 1), shift(down_after[middle:], "x", -1)]
    before[2], after[2], near, down_far = lax.optimization_barrier(
        (before[2], after[2], near, down_far)
    )

    across = jnp.concatenate([down_weight, down_after, *down_far, down_before], 0)
    down_most = lax.all_gather(across, "z", axis=0, tiled=True)

    before.append(shift(before[2], "z", 1))
    after.append(shift(after[2], "z", -1))
    near = jnp.stack(near, 0)
    other = shift(near, "c", 1)
    far = [shift(before[3][:middle], "z", 1), shift(after[3][middle:], "z", -1)]
    parts = after + far + before[:0:-1]
    around, terms = forward_terms(place, own, near, other, gathered, parts)

    def arranged(values):
        values = rolled(values.reshape(own_rows, NX, NZ, depth), 1, at_x)
        return jnp.swapaxes(values, 1, 2).reshape(own_rows, width)

    start = (at_y * NC + at_c) * own_rows
    own_tokens, own_targets = (
        arranged(lax.dynamic_slice_in_dim(a, start, own_rows, 0)) for a in (tokens, targets)
    )
    turned = rolled(around.reshape(NX * rows, slab).T.reshape(NZ, depth, NX * rows), 0, at_z)
    gram = jnp.sum(krylov[:, None] * krylov[None], axis=(2, 3)).reshape(-1)
    fifth = jnp.stack(ring_gather(gathered[:, 2 * span :], "x"), 0)
    fifth = jnp.swapaxes(fifth.reshape(NX, NZ, depth, span - cut), 0, 1)
    fifth = fifth.reshape(width, span - cut)

    forward = ring_sum([terms[d] for d in range(NX)], "x")
    gate, upward, tangent = jnp.split(forward, 3, axis=1)
    activated, derivative, curvature = gelu_parts(gate)
    hidden = (activated * upward).astype(BF16)
    hidden_tangent = (derivative * tangent * upward).astype(BF16)
    both = jnp.stack(
        [a.reshape(NC, NY, own_rows, span) for a in (hidden, hidden_tangent)], 2
    ).reshape(NC, NY * 2 * own_rows, span)

    both, down_most, fifth, turned, gram, own_tokens, own_targets = lax.optimization_barrier(
        (both, down_most, fifth, turned, gram, own_tokens, own_targets)
    )

    theirs = shift(partial_outputs(both[1], down_most, fifth), "c", 1)
    mine = partial_outputs(both[0], down_most, fifth)
    mine, theirs = (a.reshape(NY, 2, own_rows, width) for a in (mine, theirs))
    mine = lax.optimization_barrier([added(mine[d], theirs[d]) for d in range(NY)])
    outputs, outputs_tangent = ring_sum(mine, "y")
    residual = (own_tokens.astype(F32) + outputs - own_targets.astype(F32)).astype(BF16)
    residuals = jnp.stack([residual, outputs_tangent.astype(BF16)], 0)
    chip = jnp.stack(ring_gather(residuals, "y"), 0).reshape(NY * 2 * own_rows, width)
    other = shift(chip, "c", 1)
    backs = jnp.stack(
        [
            jnp.concatenate(
                [
                    jnp.dot(part, columns, preferred_element_type=F32)
                    for columns in (down_most, fifth)
                ],
                1,
            ).reshape(NY, 2, own_rows, span)
            for part in (chip, other)
        ],
        0,
    )
    backward = backs[:, :, 0].reshape(rows, span)
    backward_tangent = backs[:, :, 1].reshape(rows, span)
    gate_tangent = (
        (backward_tangent * derivative + backward * curvature * tangent) * upward
    ).astype(BF16)

    every = jnp.concatenate(ring_gather(gate_tangent, "x"), 0)
    blocks = [
        lax.optimization_barrier(contract(turned[d], every, 1, 0).astype(BF16))
        for d in range(NZ)
    ]
    product = ring_sum(blocks, "z") / (rows * NX * NZ)

    entries = width * span * NY * NC
    scaled = product / 4096.0
    sums = jnp.concatenate(
        [
            jnp.sum(krylov * product[None], axis=(1, 2)),
            gram,
            jnp.sum(scaled * scaled).reshape(1),
        ]
    )
    next_vector, row = finish(float(entries), exchanged(sums), product, krylov)
    return (next_vector, row[0, : KRYLOV + 1])


def solution(mesh):
    split = Mesh(mesh.devices.reshape(NX, NZ, NY, NC), ("x", "z", "y", "c"))
    dp, mp = ("x", "z"), ("y", "c")
    placed = (
        P(dp, None),
        P(dp, None),
        P(dp, mp),
        P(dp, mp),
        P(dp, mp),
        P(None, dp, mp),
    )
    return jax.shard_map(
        local, mesh=split, in_specs=placed, out_specs=(P(dp, mp), P()), check_vma=False
    )
```

```python
import math

import jax
import jax.numpy as jnp
from jax import lax
from jax.experimental import pallas as pl
from jax.experimental.pallas import tpu as pltpu
from jax.sharding import Mesh
from jax.sharding import PartitionSpec as P

KRYLOV = 4
NX, NZ, NY, NC = 4, 8, 4, 2

root_scale = math.sqrt(2.0 / math.pi)
cubic_term = 0.044715
epsilon = 1e-06

F32 = jnp.float32
BF16 = jnp.bfloat16


def gelu_parts(values):
    inside = root_scale * (values + cubic_term * values * values * values)
    hyperbolic = jnp.tanh(inside)
    rising = root_scale * (1.0 + 3.0 * cubic_term * values * values)
    falloff = 1.0 - hyperbolic * hyperbolic
    result = 0.5 * values * (1.0 + hyperbolic)
    derivative = 0.5 * (1.0 + hyperbolic) + 0.5 * values * falloff * rising
    curvature = falloff * rising + 0.5 * values * falloff * (
        6.0 * root_scale * cubic_term * values - 2.0 * hyperbolic * rising * rising
    )
    return (result, derivative, curvature)


def contract(left, right, left_dim, right_dim):
    return lax.dot_general(
        left, right, (((left_dim,), (right_dim,)), ((), ())), preferred_element_type=F32
    )


def shift(value, axis, by):
    size = lax.axis_size(axis)
    return lax.ppermute(value, axis, [(i, (i + by) % size) for i in range(size)])


def rolled(value, dim, start):
    size = value.shape[dim]
    return lax.dynamic_slice_in_dim(jnp.concatenate([value, value], dim), start, size, dim)


def added(first, second):
    return (first.astype(F32) + second.astype(F32)).astype(BF16)


def added_front(whole, front):
    return lax.dynamic_update_slice_in_dim(whole, added(whole[: front.shape[0]], front), 0, 0)


def added_back(whole, back):
    rows = whole.shape[0] - back.shape[0]
    return lax.dynamic_update_slice_in_dim(whole, added(whole[rows:], back), rows, 0)


def ring_sum(blocks, axis):
    size = len(blocks)
    far = size // 2
    ahead = shift(blocks[far][0], axis, 1)
    behind = shift(blocks[far][1], axis, -1)
    onward = added_front(blocks[far - 1], ahead)
    backward = added_back(blocks[far + 1], behind)
    for step in range(far - 1, 0, -1):
        ahead = shift(onward, axis, 1)
        behind = shift(backward, axis, -1)
        if step > 1:
            onward = added(blocks[step - 1], ahead)
            backward = added(blocks[size - step + 1], behind)
    return blocks[0].astype(F32) + ahead.astype(F32) + behind.astype(F32)


def ring_gather(own, axis):
    far = lax.axis_size(axis) // 2
    half = own.shape[0] // 2
    before, after = [own], [own]
    for _ in range(1, far):
        before.append(shift(before[-1], axis, 1))
        after.append(shift(after[-1], axis, -1))
    farthest = [shift(before[-1][:half], axis, 1), shift(after[-1][half:], axis, -1)]
    return after + farthest + before[:0:-1]


def exchanged(value):
    devices = NX * NZ * NY * NC
    mine = jnp.zeros((128,), F32).at[: value.shape[0]].set(value)
    return lax.all_to_all(
        jnp.broadcast_to(mine, (devices, 128)), ("x", "z", "y", "c"), 0, 0, tiled=True
    )


VMEM = pl.BlockSpec(memory_space=pltpu.VMEM)
SMEM = pl.BlockSpec(memory_space=pltpu.SMEM)
LIMIT = pltpu.CompilerParams(vmem_limit_bytes=40 * 1024 * 1024)


def norm_kernel(place, tokens, own, *rest):
    sent, held = rest[: NX - 1], rest[NX - 1]
    count = held.shape[0]
    slab = own.shape[1]
    at_x, at_y, at_c = place[0], place[1], place[2]
    for c in range(NC):
        for y in range(NY):
            group = lax.rem(at_y + y, NY) * NC + lax.rem(at_c + c, NC)
            start = pl.multiple_of(group * count, count)
            values = tokens[pl.ds(start, count), :].astype(F32)
            square = jnp.mean(values * values, axis=1, keepdims=True)
            held[...] = (values * lax.rsqrt(square + epsilon)).astype(BF16)
            at = pl.ds((c * NY + y) * count, count)
            for ahead in range(NX if c == 0 else 1):
                columns = pl.ds(pl.multiple_of(lax.rem(at_x + ahead, NX) * slab, slab), slab)
                target = own if ahead == 0 else sent[ahead - 1]
                target[at, :] = held[:, columns]


def norm_tokens(place, tokens):
    rows, width = tokens.shape
    slab = width // NX
    shapes = [jax.ShapeDtypeStruct((rows, slab), BF16)]
    shapes += [jax.ShapeDtypeStruct((rows // NC, slab), BF16)] * (NX - 1)
    return pl.pallas_call(
        norm_kernel,
        out_shape=shapes,
        in_specs=[SMEM, VMEM],
        out_specs=[VMEM] * NX,
        scratch_shapes=[pltpu.VMEM((rows // (NC * NY), width), BF16)],
        compiler_params=LIMIT,
        cost_estimate=pl.CostEstimate(
            flops=4 * rows * width, bytes_accessed=4 * rows * width, transcendentals=rows
        ),
    )(place, tokens)


def forward_kernel(place, own, near, other, gathered, *rest):
    parts, (around, terms, matrix, pair, arrived) = rest[: NZ + 1], rest[NZ + 1 :]
    depth = parts[0].shape[0]
    half = near.shape[1]
    two = pair.shape[1]
    moves = [(own, around.at[0]), (gathered.at[:, :two], pair)]
    for d in range(1, NX):
        moves.append((near.at[d - 1], around.at[d, :half]))
        moves.append((other.at[d - 1], around.at[d, half:]))
    at = 0
    for part in parts:
        count = part.shape[0]
        ahead, offset = at // depth, at % depth
        start = lax.rem(place[3] + ahead, NZ) * depth + offset
        moves.append((part, matrix.at[pl.ds(pl.multiple_of(start, count), count)]))
        at += count
    copies = [
        pltpu.make_async_copy(source, target, arrived.at[i])
        for i, (source, target) in enumerate(moves)
    ]
    for copy in copies:
        copy.start()
    for copy in copies:
        copy.wait()
    for d in range(NX):
        terms[d, :, :two] = jnp.dot(around[d], pair[...], preferred_element_type=F32).astype(BF16)
        terms[d, :, two:] = jnp.dot(
            around[d], matrix[...], preferred_element_type=F32
        ).astype(BF16)


def forward_terms(place, own, near, other, gathered, parts):
    rows, slab = own.shape
    span = parts[0].shape[1]
    width = 3 * span
    anywhere = pl.BlockSpec(memory_space=pl.ANY)
    return pl.pallas_call(
        forward_kernel,
        out_shape=[
            jax.ShapeDtypeStruct((NX, rows, slab), BF16),
            jax.ShapeDtypeStruct((NX, rows, width), BF16),
        ],
        in_specs=[SMEM] + [anywhere] * (4 + len(parts)),
        out_specs=[VMEM] * 2,
        scratch_shapes=[
            pltpu.VMEM((slab, span), BF16),
            pltpu.VMEM((slab, 2 * span), BF16),
            pltpu.SemaphoreType.DMA((2 + 2 * (NX - 1) + len(parts),)),
        ],
        compiler_params=LIMIT,
        cost_estimate=pl.CostEstimate(
            flops=2 * NX * rows * slab * width,
            bytes_accessed=2 * (2 * NX * rows * slab + slab * width + NX * rows * width),
            transcendentals=0,
        ),
    )(place, own, near, other, gathered, *parts)


def partial_kernel(units, down, partial):
    partial[...] = contract(units[...], down[...], 1, 1).astype(BF16)


def partial_outputs(units, down):
    rows, span = units.shape
    width = down.shape[0]
    slab = width // NX
    return pl.pallas_call(
        partial_kernel,
        grid=(NX,),
        out_shape=jax.ShapeDtypeStruct((rows, width), BF16),
        in_specs=[
            pl.BlockSpec((rows, span), lambda i: (0, 0)),
            pl.BlockSpec((slab, span), lambda i: (i, 0)),
        ],
        out_specs=pl.BlockSpec((rows, slab), lambda i: (0, i)),
        compiler_params=LIMIT,
        cost_estimate=pl.CostEstimate(
            flops=2 * rows * span * width,
            bytes_accessed=2 * (rows * span + width * span + rows * width),
            transcendentals=0,
        ),
    )(units, down)


def beside_kernel(left, right, both, arrived):
    span = left.shape[1]
    copies = [
        pltpu.make_async_copy(left, both.at[:, :span], arrived.at[0]),
        pltpu.make_async_copy(right, both.at[:, span:], arrived.at[1]),
    ]
    for copy in copies:
        copy.start()
    for copy in copies:
        copy.wait()


def beside(left, right):
    rows, span = left.shape
    anywhere = pl.BlockSpec(memory_space=pl.ANY)
    return pl.pallas_call(
        beside_kernel,
        out_shape=jax.ShapeDtypeStruct((rows, 2 * span), BF16),
        in_specs=[anywhere] * 2,
        out_specs=anywhere,
        scratch_shapes=[pltpu.SemaphoreType.DMA((2,))],
        compiler_params=LIMIT,
        cost_estimate=pl.CostEstimate(
            flops=0, bytes_accessed=8 * rows * span, transcendentals=0
        ),
    )(left, right)


def product_kernel(turned, *rest):
    parts, targets, every = rest[: NX + 1], rest[NX + 1 : -1], rest[-1]
    at = 0
    for part in parts:
        every[at : at + part.shape[0], :] = part[...]
        at += part.shape[0]
    depth = turned.shape[1]
    for pair in range(0, NZ, 2):
        rows = turned[pair : pair + 2].reshape(2 * depth, every.shape[0])
        values = jnp.dot(rows, every[...], preferred_element_type=F32).astype(BF16)
        if pair == NZ // 2:
            pieces = [targets[pair], targets[pair + 1], targets[pair + 2]]
        else:
            pieces = targets[pair + (pair > NZ // 2) :][:2]
        at = 0
        for target in pieces:
            target[...] = values[at : at + target.shape[0]]
            at += target.shape[0]


def product_terms(turned, parts):
    depth, span = turned.shape[1], parts[0].shape[1]
    counts = [depth] * NZ
    counts[NZ // 2 : NZ // 2 + 1] = [depth // 2] * 2
    return pl.pallas_call(
        product_kernel,
        out_shape=[jax.ShapeDtypeStruct((count, span), BF16) for count in counts],
        in_specs=[VMEM] * (1 + len(parts)),
        out_specs=[VMEM] * len(counts),
        scratch_shapes=[pltpu.VMEM((turned.shape[2], span), BF16)],
        compiler_params=LIMIT,
        cost_estimate=pl.CostEstimate(
            flops=2 * turned.size * span,
            bytes_accessed=2 * (turned.size + (turned.shape[2] + NZ * depth) * span),
            transcendentals=0,
        ),
    )(turned, *parts)


def end_kernel(entries, every, product, krylov, vector, coefficients):
    sums = jnp.sum(every[...], axis=0, keepdims=True)
    lane = lax.broadcasted_iota(jnp.int32, sums.shape, 1)

    def at(place):
        return jnp.sum(jnp.where(lane == place, sums, 0.0), axis=1, keepdims=True)

    projections = [at(i) / entries for i in range(KRYLOV)]
    mean_square = at(KRYLOV + KRYLOV * KRYLOV) * (4096.0 * 4096.0 / entries)
    for i in range(KRYLOV):
        mean_square -= 2.0 * projections[i] * projections[i]
    for i in range(KRYLOV):
        for j in range(KRYLOV):
            gram = at(KRYLOV + KRYLOV * i + j) / entries
            mean_square += projections[i] * projections[j] * gram
    norm_value = jnp.sqrt(jnp.maximum(mean_square, 0.0) + epsilon)
    row = jnp.where(lane == KRYLOV, norm_value, 0.0)
    projected = product[...]
    for i in range(KRYLOV):
        projected -= projections[i] * krylov[i]
        row = jnp.where(lane == i, projections[i], row)
    vector[...] = projected / norm_value
    coefficients[...] = row


def finish(entries, every, product, krylov):
    return pl.pallas_call(
        lambda *refs: end_kernel(entries, *refs),
        out_shape=[
            jax.ShapeDtypeStruct(product.shape, F32),
            jax.ShapeDtypeStruct((1, every.shape[1]), F32),
        ],
        in_specs=[VMEM] * 3,
        out_specs=[VMEM] * 2,
        compiler_params=LIMIT,
        cost_estimate=pl.CostEstimate(
            flops=10 * product.size, bytes_accessed=24 * product.size, transcendentals=1
        ),
    )(every, product, krylov)


def local(tokens, targets, gate_weight, up_weight, down_weight, krylov):
    rows, width = tokens.shape
    depth, span = gate_weight.shape
    own_rows = rows // (NY * NC)
    slab = width // NX
    at_x, at_z, at_y, at_c = (lax.axis_index(name) for name in ("x", "z", "y", "c"))

    gathered = lax.all_gather(beside(gate_weight, up_weight), "z", axis=0, tiled=True)
    direction = krylov[KRYLOV - 1].astype(BF16)
    before, after = [direction], [direction]
    before.append(shift(direction, "z", 1))
    after.append(shift(direction, "z", -1))
    down_before, down_after = shift(down_weight, "x", 1), shift(down_weight, "x", -1)

    place = jnp.stack([at_x, at_y, at_c, at_z]).astype(jnp.int32)
    own, *sent = norm_tokens(place, tokens)
    before[1], after[1], down_before, down_after = lax.optimization_barrier(
        (before[1], after[1], down_before, down_after)
    )
    before.append(shift(before[1], "z", 1))
    after.append(shift(after[1], "z", -1))
    middle = depth // 2
    down_far = [shift(down_before[:middle], "x", 1), shift(down_after[middle:], "x", -1)]
    down_far, own, sent = lax.optimization_barrier((down_far, own, sent))
    near = [shift(sent[ahead - 1], "x", ahead) for ahead in range(NX - 1, 0, -1)]
    before[2], after[2], near = lax.optimization_barrier((before[2], after[2], near))

    across = jnp.concatenate([down_weight, down_after, *down_far, down_before], 0)
    down_full = lax.all_gather(across, "z", axis=0, tiled=True)

    before.append(shift(before[2], "z", 1))
    after.append(shift(after[2], "z", -1))
    near = jnp.stack(near, 0)
    other = shift(near, "c", 1)
    far = [shift(before[3][:middle], "z", 1), shift(after[3][middle:], "z", -1)]
    parts = after + far + before[:0:-1]
    around, terms = forward_terms(place, own, near, other, gathered, parts)

    def arranged(values):
        values = rolled(values.reshape(own_rows, NX, NZ, depth), 1, at_x)
        return jnp.swapaxes(values, 1, 2).reshape(own_rows, width)

    start = (at_y * NC + at_c) * own_rows
    own_tokens, own_targets = (
        arranged(lax.dynamic_slice_in_dim(a, start, own_rows, 0)) for a in (tokens, targets)
    )
    turned = rolled(around.reshape(NX * rows, slab).T.reshape(NZ, depth, NX * rows), 0, at_z)
    gram = jnp.sum(krylov[:, None] * krylov[None], axis=(2, 3)).reshape(-1)
    halves = (terms[2, : rows // 2], terms[2, rows // 2 :])
    forward = ring_sum([terms[0], terms[1], halves, terms[3]], "x")
    gate, upward, tangent = jnp.split(forward, 3, axis=1)
    activated, derivative, curvature = gelu_parts(gate)
    hidden = (activated * upward).astype(BF16)
    hidden_tangent = (derivative * tangent * upward).astype(BF16)
    kinds = [a.reshape(NC, NY, own_rows, span) for a in (hidden, hidden_tangent)]
    ours, yours = (
        jnp.stack([a[c] for a in kinds], 1).reshape(NY * 2 * own_rows, span) for c in range(NC)
    )
    ours, yours, down_full, turned, gram, own_tokens, own_targets = lax.optimization_barrier(
        (ours, yours, down_full, turned, gram, own_tokens, own_targets)
    )

    theirs = shift(partial_outputs(yours, down_full), "c", 1)
    mine = lax.optimization_barrier(contract(ours, down_full, 1, 1).astype(BF16))
    mine, theirs = (a.reshape(NY, 2, own_rows, width) for a in (mine, theirs))
    mine = lax.optimization_barrier([added(mine[d], theirs[d]) for d in range(NY)])
    mine[2] = (mine[2][:1], mine[2][1:])
    outputs, outputs_tangent = ring_sum(mine, "y")
    residual = (own_tokens.astype(F32) + outputs - own_targets.astype(F32)).astype(BF16)
    residuals = jnp.stack([residual, outputs_tangent.astype(BF16)], 0)
    chip = jnp.concatenate(ring_gather(residuals, "y"), 0).reshape(NY * 2 * own_rows, width)
    other = shift(chip, "c", 1)
    backs = jnp.stack(
        [
            jnp.dot(part, down_full, preferred_element_type=F32).reshape(NY, 2, own_rows, span)
            for part in (chip, other)
        ],
        0,
    )
    backward = backs[:, :, 0].reshape(rows, span)
    backward_tangent = backs[:, :, 1].reshape(rows, span)
    gate_tangent = (
        (backward_tangent * derivative + backward * curvature * tangent) * upward
    ).astype(BF16)

    blocks = list(product_terms(turned, ring_gather(gate_tangent, "x")))
    blocks[NZ // 2 : NZ // 2 + 2] = [tuple(blocks[NZ // 2 : NZ // 2 + 2])]
    product = ring_sum(blocks, "z") / (rows * NX * NZ)

    entries = width * span * NY * NC
    scaled = product / 4096.0
    sums = jnp.concatenate(
        [
            jnp.sum(krylov * product[None], axis=(1, 2)),
            gram,
            jnp.sum(scaled * scaled).reshape(1),
        ]
    )
    next_vector, row = finish(float(entries), exchanged(sums), product, krylov)
    return (next_vector, row[0, : KRYLOV + 1])


def solution(mesh):
    split = Mesh(mesh.devices.reshape(NX, NZ, NY, NC), ("x", "z", "y", "c"))
    dp, mp = ("x", "z"), ("y", "c")
    placed = (
        P(dp, None),
        P(dp, None),
        P(dp, mp),
        P(dp, mp),
        P(dp, mp),
        P(None, dp, mp),
    )
    return jax.shard_map(
        local, mesh=split, in_specs=placed, out_specs=(P(dp, mp), P()), check_vma=False
    )
```

```python
import math

import jax
import jax.numpy as jnp
from jax import lax
from jax.experimental import pallas as pl
from jax.experimental.pallas import tpu as pltpu
from jax.sharding import Mesh
from jax.sharding import PartitionSpec as P

KRYLOV = 4
NX, NZ, NY, NC = 4, 8, 4, 2

root_scale = math.sqrt(2.0 / math.pi)
cubic_term = 0.044715
epsilon = 1e-06

F32 = jnp.float32
BF16 = jnp.bfloat16


def gelu_parts(values):
    inside = root_scale * (values + cubic_term * values * values * values)
    hyperbolic = jnp.tanh(inside)
    rising = root_scale * (1.0 + 3.0 * cubic_term * values * values)
    falloff = 1.0 - hyperbolic * hyperbolic
    result = 0.5 * values * (1.0 + hyperbolic)
    derivative = 0.5 * (1.0 + hyperbolic) + 0.5 * values * falloff * rising
    curvature = falloff * rising + 0.5 * values * falloff * (
        6.0 * root_scale * cubic_term * values - 2.0 * hyperbolic * rising * rising
    )
    return (result, derivative, curvature)


def contract(left, right, left_dim, right_dim):
    return lax.dot_general(
        left, right, (((left_dim,), (right_dim,)), ((), ())), preferred_element_type=F32
    )


def shift(value, axis, by):
    size = lax.axis_size(axis)
    return lax.ppermute(value, axis, [(i, (i + by) % size) for i in range(size)])


def rolled(value, dim, start):
    size = value.shape[dim]
    return lax.dynamic_slice_in_dim(jnp.concatenate([value, value], dim), start, size, dim)


def added(first, second):
    return (first.astype(F32) + second.astype(F32)).astype(BF16)


def added_front(whole, front):
    return lax.dynamic_update_slice_in_dim(whole, added(whole[: front.shape[0]], front), 0, 0)


def added_back(whole, back):
    rows = whole.shape[0] - back.shape[0]
    return lax.dynamic_update_slice_in_dim(whole, added(whole[rows:], back), rows, 0)


def ring_sum(blocks, axis):
    size = len(blocks)
    far = size // 2
    half = blocks[far].shape[0] // 2
    ahead = shift(blocks[far][:half], axis, 1)
    behind = shift(blocks[far][half:], axis, -1)
    onward = added_front(blocks[far - 1], ahead)
    backward = added_back(blocks[far + 1], behind)
    for step in range(far - 1, 0, -1):
        ahead = shift(onward, axis, 1)
        behind = shift(backward, axis, -1)
        if step > 1:
            onward = added(blocks[step - 1], ahead)
            backward = added(blocks[size - step + 1], behind)
    return blocks[0].astype(F32) + ahead.astype(F32) + behind.astype(F32)


def ring_gather(own, axis):
    far = lax.axis_size(axis) // 2
    half = own.shape[0] // 2
    before, after = [own], [own]
    for _ in range(1, far):
        before.append(shift(before[-1], axis, 1))
        after.append(shift(after[-1], axis, -1))
    farthest = jnp.concatenate(
        [shift(before[-1][:half], axis, 1), shift(after[-1][half:], axis, -1)], 0
    )
    return after + [farthest] + before[:0:-1]


def exchanged(value):
    devices = NX * NZ * NY * NC
    mine = jnp.zeros((128,), F32).at[: value.shape[0]].set(value)
    return lax.all_to_all(
        jnp.broadcast_to(mine, (devices, 128)), ("x", "z", "y", "c"), 0, 0, tiled=True
    )


VMEM = pl.BlockSpec(memory_space=pltpu.VMEM)
SMEM = pl.BlockSpec(memory_space=pltpu.SMEM)
LIMIT = pltpu.CompilerParams(vmem_limit_bytes=40 * 1024 * 1024)


def norm_kernel(place, tokens, own, *rest):
    sent, held = rest[: NX - 1], rest[NX - 1]
    count = held.shape[0]
    slab = own.shape[1]
    at_x, at_y, at_c = place[0], place[1], place[2]
    for c in range(NC):
        for y in range(NY):
            group = lax.rem(at_y + y, NY) * NC + lax.rem(at_c + c, NC)
            start = pl.multiple_of(group * count, count)
            values = tokens[pl.ds(start, count), :].astype(F32)
            square = jnp.mean(values * values, axis=1, keepdims=True)
            held[...] = (values * lax.rsqrt(square + epsilon)).astype(BF16)
            at = pl.ds((c * NY + y) * count, count)
            for ahead in range(NX if c == 0 else 1):
                columns = pl.ds(pl.multiple_of(lax.rem(at_x + ahead, NX) * slab, slab), slab)
                target = own if ahead == 0 else sent[ahead - 1]
                target[at, :] = held[:, columns]


def norm_tokens(place, tokens):
    rows, width = tokens.shape
    slab = width // NX
    shapes = [jax.ShapeDtypeStruct((rows, slab), BF16)]
    shapes += [jax.ShapeDtypeStruct((rows // NC, slab), BF16)] * (NX - 1)
    return pl.pallas_call(
        norm_kernel,
        out_shape=shapes,
        in_specs=[SMEM, VMEM],
        out_specs=[VMEM] * NX,
        scratch_shapes=[pltpu.VMEM((rows // (NC * NY), width), BF16)],
        compiler_params=LIMIT,
        cost_estimate=pl.CostEstimate(
            flops=4 * rows * width, bytes_accessed=4 * rows * width, transcendentals=rows
        ),
    )(place, tokens)


def forward_kernel(place, own, near, other, gathered, *rest):
    parts, (around, terms, matrix) = rest[: NZ + 1], rest[NZ + 1 :]
    depth = parts[0].shape[0]
    half = near.shape[1]
    two = gathered.shape[1]
    at = 0
    for part in parts:
        count = part.shape[0]
        ahead, offset = at // depth, at % depth
        start = lax.rem(place[3] + ahead, NZ) * depth + offset
        matrix[pl.ds(pl.multiple_of(start, count), count), :] = part[...]
        at += count
    around[0] = own[...]
    for d in range(1, NX):
        around[d, :half, :] = near[d - 1]
        around[d, half:, :] = other[d - 1]
    for d in range(NX):
        terms[d, :, :two] = jnp.dot(
            around[d], gathered[...], preferred_element_type=F32
        ).astype(BF16)
        terms[d, :, two:] = jnp.dot(
            around[d], matrix[...], preferred_element_type=F32
        ).astype(BF16)


def forward_terms(place, own, near, other, gathered, parts):
    rows, slab = own.shape
    span = parts[0].shape[1]
    width = gathered.shape[1] + span
    return pl.pallas_call(
        forward_kernel,
        out_shape=[
            jax.ShapeDtypeStruct((NX, rows, slab), BF16),
            jax.ShapeDtypeStruct((NX, rows, width), BF16),
        ],
        in_specs=[SMEM] + [VMEM] * (4 + len(parts)),
        out_specs=[VMEM] * 2,
        scratch_shapes=[pltpu.VMEM((slab, span), BF16)],
        compiler_params=LIMIT,
        cost_estimate=pl.CostEstimate(
            flops=2 * NX * rows * slab * width,
            bytes_accessed=2 * (2 * NX * rows * slab + slab * width + NX * rows * width),
            transcendentals=0,
        ),
    )(place, own, near, other, gathered, *parts)


def end_kernel(entries, every, product, krylov, vector, coefficients):
    sums = jnp.sum(every[...], axis=0, keepdims=True)
    lane = lax.broadcasted_iota(jnp.int32, sums.shape, 1)

    def at(place):
        return jnp.sum(jnp.where(lane == place, sums, 0.0), axis=1, keepdims=True)

    projections = [at(i) / entries for i in range(KRYLOV)]
    mean_square = at(KRYLOV + KRYLOV * KRYLOV) * (4096.0 * 4096.0 / entries)
    for i in range(KRYLOV):
        mean_square -= 2.0 * projections[i] * projections[i]
    for i in range(KRYLOV):
        for j in range(KRYLOV):
            gram = at(KRYLOV + KRYLOV * i + j) / entries
            mean_square += projections[i] * projections[j] * gram
    norm_value = jnp.sqrt(jnp.maximum(mean_square, 0.0) + epsilon)
    row = jnp.where(lane == KRYLOV, norm_value, 0.0)
    projected = product[...]
    for i in range(KRYLOV):
        projected -= projections[i] * krylov[i]
        row = jnp.where(lane == i, projections[i], row)
    vector[...] = projected / norm_value
    coefficients[...] = row


def finish(entries, every, product, krylov):
    return pl.pallas_call(
        lambda *refs: end_kernel(entries, *refs),
        out_shape=[
            jax.ShapeDtypeStruct(product.shape, F32),
            jax.ShapeDtypeStruct((1, every.shape[1]), F32),
        ],
        in_specs=[VMEM] * 3,
        out_specs=[VMEM] * 2,
        compiler_params=LIMIT,
        cost_estimate=pl.CostEstimate(
            flops=10 * product.size, bytes_accessed=24 * product.size, transcendentals=1
        ),
    )(every, product, krylov)


def local(tokens, targets, gate_weight, up_weight, down_weight, krylov):
    rows, width = tokens.shape
    depth, span = gate_weight.shape
    own_rows = rows // (NY * NC)
    slab = width // NX
    at_x, at_z, at_y, at_c = (lax.axis_index(name) for name in ("x", "z", "y", "c"))

    gathered = lax.all_gather(
        jnp.concatenate([gate_weight, up_weight], 1), "z", axis=0, tiled=True
    )
    direction = krylov[KRYLOV - 1].astype(BF16)
    before, after = [direction], [direction]
    before.append(shift(direction, "z", 1))
    after.append(shift(direction, "z", -1))
    down_before, down_after = shift(down_weight, "x", 1), shift(down_weight, "x", -1)

    place = jnp.stack([at_x, at_y, at_c, at_z]).astype(jnp.int32)
    own, *sent = norm_tokens(place, tokens)
    before[1], after[1], down_before, down_after, own, sent = lax.optimization_barrier(
        (before[1], after[1], down_before, down_after, own, sent)
    )
    near = [shift(sent[ahead - 1], "x", ahead) for ahead in range(NX - 1, 0, -1)]
    before.append(shift(before[1], "z", 1))
    after.append(shift(after[1], "z", -1))
    middle = depth // 2
    down_far = [shift(down_before[:middle], "x", 1), shift(down_after[middle:], "x", -1)]
    before[2], after[2], near, down_far = lax.optimization_barrier(
        (before[2], after[2], near, down_far)
    )

    across = jnp.concatenate([down_weight, down_after, *down_far, down_before], 0)
    down_full = lax.all_gather(across, "z", axis=0, tiled=True)

    before.append(shift(before[2], "z", 1))
    after.append(shift(after[2], "z", -1))
    near = jnp.stack(near, 0)
    other = shift(near, "c", 1)
    far = [shift(before[3][:middle], "z", 1), shift(after[3][middle:], "z", -1)]
    parts = after + far + before[:0:-1]
    around, terms = forward_terms(place, own, near, other, gathered, parts)

    def arranged(values):
        values = rolled(values.reshape(own_rows, NX, NZ, depth), 1, at_x)
        return jnp.swapaxes(values, 1, 2).reshape(own_rows, width)

    start = (at_y * NC + at_c) * own_rows
    own_tokens, own_targets = (
        arranged(lax.dynamic_slice_in_dim(a, start, own_rows, 0)) for a in (tokens, targets)
    )
    turned = rolled(around.reshape(NX * rows, slab).T.reshape(NZ, depth, NX * rows), 0, at_z)
    gram = jnp.sum(krylov[:, None] * krylov[None], axis=(2, 3)).reshape(-1)
    forward = ring_sum([terms[d] for d in range(NX)], "x")
    gate, upward, tangent = jnp.split(forward, 3, axis=1)
    activated, derivative, curvature = gelu_parts(gate)
    hidden = (activated * upward).astype(BF16)
    hidden_tangent = (derivative * tangent * upward).astype(BF16)
    both = jnp.stack(
        [a.reshape(NC, NY, own_rows, span) for a in (hidden, hidden_tangent)], 2
    ).reshape(NC, NY * 2 * own_rows, span)

    both, down_full, turned, gram, own_tokens, own_targets = lax.optimization_barrier(
        (both, down_full, turned, gram, own_tokens, own_targets)
    )

    theirs = shift(contract(both[1], down_full, 1, 1).astype(BF16), "c", 1)
    mine = lax.optimization_barrier(contract(both[0], down_full, 1, 1).astype(BF16))
    mine, theirs = (a.reshape(NY, 2, own_rows, width) for a in (mine, theirs))
    mine = lax.optimization_barrier(
        [[added(mine[d, kind], theirs[d, kind]) for d in range(NY)] for kind in range(2)]
    )
    outputs, outputs_tangent = (ring_sum(blocks, "y") for blocks in mine)
    residual = (own_tokens.astype(F32) + outputs - own_targets.astype(F32)).astype(BF16)
    kinds = [ring_gather(a, "y") for a in (residual, outputs_tangent.astype(BF16))]
    chip = jnp.concatenate([kinds[kind][d] for d in range(NY) for kind in range(2)], 0)
    other = shift(chip, "c", 1)
    backs = jnp.stack(
        [
            jnp.dot(part, down_full, preferred_element_type=F32).reshape(NY, 2, own_rows, span)
            for part in (chip, other)
        ],
        0,
    )
    backward = backs[:, :, 0].reshape(rows, span)
    backward_tangent = backs[:, :, 1].reshape(rows, span)
    gate_tangent = (
        (backward_tangent * derivative + backward * curvature * tangent) * upward
    ).astype(BF16)

    every = jnp.concatenate(ring_gather(gate_tangent, "x"), 0)
    blocks = [
        lax.optimization_barrier(contract(turned[d], every, 1, 0).astype(BF16))
        for d in range(NZ)
    ]
    product = ring_sum(blocks, "z") / (rows * NX * NZ)

    entries = width * span * NY * NC
    scaled = product / 4096.0
    sums = jnp.concatenate(
        [
            jnp.sum(krylov * product[None], axis=(1, 2)),
            gram,
            jnp.sum(scaled * scaled).reshape(1),
        ]
    )
    next_vector, row = finish(float(entries), exchanged(sums), product, krylov)
    return (next_vector, row[0, : KRYLOV + 1])


def solution(mesh):
    split = Mesh(mesh.devices.reshape(NX, NZ, NY, NC), ("x", "z", "y", "c"))
    dp, mp = ("x", "z"), ("y", "c")
    placed = (
        P(dp, None),
        P(dp, None),
        P(dp, mp),
        P(dp, mp),
        P(dp, mp),
        P(None, dp, mp),
    )
    return jax.shard_map(
        local, mesh=split, in_specs=placed, out_specs=(P(dp, mp), P()), check_vma=False
    )
```

```python
import math

import jax
import jax.numpy as jnp
from jax import lax
from jax.experimental import pallas as pl
from jax.experimental.pallas import tpu as pltpu
from jax.sharding import Mesh
from jax.sharding import PartitionSpec as P

KRYLOV = 4
NX, NZ, NY, NC = 4, 8, 4, 2

root_scale = math.sqrt(2.0 / math.pi)
cubic_term = 0.044715
epsilon = 1e-06

F32 = jnp.float32
BF16 = jnp.bfloat16


def gelu_parts(values):
    inside = root_scale * (values + cubic_term * values * values * values)
    hyperbolic = jnp.tanh(inside)
    rising = root_scale * (1.0 + 3.0 * cubic_term * values * values)
    falloff = 1.0 - hyperbolic * hyperbolic
    result = 0.5 * values * (1.0 + hyperbolic)
    derivative = 0.5 * (1.0 + hyperbolic) + 0.5 * values * falloff * rising
    curvature = falloff * rising + 0.5 * values * falloff * (
        6.0 * root_scale * cubic_term * values - 2.0 * hyperbolic * rising * rising
    )
    return (result, derivative, curvature)


def contract(left, right, left_dim, right_dim):
    return lax.dot_general(
        left, right, (((left_dim,), (right_dim,)), ((), ())), preferred_element_type=F32
    )


def shift(value, axis, by):
    size = lax.axis_size(axis)
    return lax.ppermute(value, axis, [(i, (i + by) % size) for i in range(size)])


def rolled(value, dim, start):
    size = value.shape[dim]
    return lax.dynamic_slice_in_dim(jnp.concatenate([value, value], dim), start, size, dim)


def added(first, second):
    return (first.astype(F32) + second.astype(F32)).astype(BF16)


def added_front(whole, front):
    return lax.dynamic_update_slice_in_dim(whole, added(whole[: front.shape[0]], front), 0, 0)


def added_back(whole, back):
    rows = whole.shape[0] - back.shape[0]
    return lax.dynamic_update_slice_in_dim(whole, added(whole[rows:], back), rows, 0)


def ring_sum(blocks, axis):
    size = len(blocks)
    far = size // 2
    half = blocks[far].shape[0] // 2
    ahead = shift(blocks[far][:half], axis, 1)
    behind = shift(blocks[far][half:], axis, -1)
    onward = added_front(blocks[far - 1], ahead)
    backward = added_back(blocks[far + 1], behind)
    for step in range(far - 1, 0, -1):
        ahead = shift(onward, axis, 1)
        behind = shift(backward, axis, -1)
        if step > 1:
            onward = added(blocks[step - 1], ahead)
            backward = added(blocks[size - step + 1], behind)
    return blocks[0].astype(F32) + ahead.astype(F32) + behind.astype(F32)


def ring_gather(own, axis):
    far = lax.axis_size(axis) // 2
    half = own.shape[0] // 2
    before, after = [own], [own]
    for _ in range(1, far):
        before.append(shift(before[-1], axis, 1))
        after.append(shift(after[-1], axis, -1))
    farthest = jnp.concatenate(
        [shift(before[-1][:half], axis, 1), shift(after[-1][half:], axis, -1)], 0
    )
    return after + [farthest] + before[:0:-1]


def exchanged(value):
    devices = NX * NZ * NY * NC
    mine = jnp.zeros((128,), F32).at[: value.shape[0]].set(value)
    return lax.all_to_all(
        jnp.broadcast_to(mine, (devices, 128)), ("x", "z", "y", "c"), 0, 0, tiled=True
    )


VMEM = pl.BlockSpec(memory_space=pltpu.VMEM)
SMEM = pl.BlockSpec(memory_space=pltpu.SMEM)
LIMIT = pltpu.CompilerParams(vmem_limit_bytes=40 * 1024 * 1024)


def norm_kernel(place, tokens, own, *rest):
    sent, held = rest[: NX - 1], rest[NX - 1]
    count = held.shape[0]
    slab = own.shape[1]
    at_x, at_y, at_c = place[0], place[1], place[2]
    for c in range(NC):
        for y in range(NY):
            group = lax.rem(at_y + y, NY) * NC + lax.rem(at_c + c, NC)
            start = pl.multiple_of(group * count, count)
            values = tokens[pl.ds(start, count), :].astype(F32)
            square = jnp.mean(values * values, axis=1, keepdims=True)
            held[...] = (values * lax.rsqrt(square + epsilon)).astype(BF16)
            at = pl.ds((c * NY + y) * count, count)
            for ahead in range(NX if c == 0 else 1):
                columns = pl.ds(pl.multiple_of(lax.rem(at_x + ahead, NX) * slab, slab), slab)
                target = own if ahead == 0 else sent[ahead - 1]
                target[at, :] = held[:, columns]


def norm_tokens(place, tokens):
    rows, width = tokens.shape
    slab = width // NX
    shapes = [jax.ShapeDtypeStruct((rows, slab), BF16)]
    shapes += [jax.ShapeDtypeStruct((rows // NC, slab), BF16)] * (NX - 1)
    return pl.pallas_call(
        norm_kernel,
        out_shape=shapes,
        in_specs=[SMEM, VMEM],
        out_specs=[VMEM] * NX,
        scratch_shapes=[pltpu.VMEM((rows // (NC * NY), width), BF16)],
        compiler_params=LIMIT,
        cost_estimate=pl.CostEstimate(
            flops=4 * rows * width, bytes_accessed=4 * rows * width, transcendentals=rows
        ),
    )(place, tokens)


def forward_kernel(place, own, near, other, gathered, *rest):
    parts, (around, terms, matrix) = rest[: NZ + 1], rest[NZ + 1 :]
    depth = parts[0].shape[0]
    half = near.shape[1]
    two = gathered.shape[1]
    at = 0
    for part in parts:
        count = part.shape[0]
        ahead, offset = at // depth, at % depth
        start = lax.rem(place[3] + ahead, NZ) * depth + offset
        matrix[pl.ds(pl.multiple_of(start, count), count), :] = part[...]
        at += count
    around[0] = own[...]
    for d in range(1, NX):
        around[d, :half, :] = near[d - 1]
        around[d, half:, :] = other[d - 1]
    for d in range(NX):
        terms[d, :, :two] = jnp.dot(
            around[d], gathered[...], preferred_element_type=F32
        ).astype(BF16)
        terms[d, :, two:] = jnp.dot(
            around[d], matrix[...], preferred_element_type=F32
        ).astype(BF16)


def forward_terms(place, own, near, other, gathered, parts):
    rows, slab = own.shape
    span = parts[0].shape[1]
    width = gathered.shape[1] + span
    return pl.pallas_call(
        forward_kernel,
        out_shape=[
            jax.ShapeDtypeStruct((NX, rows, slab), BF16),
            jax.ShapeDtypeStruct((NX, rows, width), BF16),
        ],
        in_specs=[SMEM] + [VMEM] * (4 + len(parts)),
        out_specs=[VMEM] * 2,
        scratch_shapes=[pltpu.VMEM((slab, span), BF16)],
        compiler_params=LIMIT,
        cost_estimate=pl.CostEstimate(
            flops=2 * NX * rows * slab * width,
            bytes_accessed=2 * (2 * NX * rows * slab + slab * width + NX * rows * width),
            transcendentals=0,
        ),
    )(place, own, near, other, gathered, *parts)


def end_kernel(entries, every, product, krylov, vector, coefficients):
    sums = jnp.sum(every[...], axis=0, keepdims=True)
    lane = lax.broadcasted_iota(jnp.int32, sums.shape, 1)

    def at(place):
        return jnp.sum(jnp.where(lane == place, sums, 0.0), axis=1, keepdims=True)

    projections = [at(i) / entries for i in range(KRYLOV)]
    mean_square = at(KRYLOV + KRYLOV * KRYLOV) * (4096.0 * 4096.0 / entries)
    for i in range(KRYLOV):
        mean_square -= 2.0 * projections[i] * projections[i]
    for i in range(KRYLOV):
        for j in range(KRYLOV):
            gram = at(KRYLOV + KRYLOV * i + j) / entries
            mean_square += projections[i] * projections[j] * gram
    norm_value = jnp.sqrt(jnp.maximum(mean_square, 0.0) + epsilon)
    row = jnp.where(lane == KRYLOV, norm_value, 0.0)
    projected = product[...]
    for i in range(KRYLOV):
        projected -= projections[i] * krylov[i]
        row = jnp.where(lane == i, projections[i], row)
    vector[...] = projected / norm_value
    coefficients[...] = row


def finish(entries, every, product, krylov):
    return pl.pallas_call(
        lambda *refs: end_kernel(entries, *refs),
        out_shape=[
            jax.ShapeDtypeStruct(product.shape, F32),
            jax.ShapeDtypeStruct((1, every.shape[1]), F32),
        ],
        in_specs=[VMEM] * 3,
        out_specs=[VMEM] * 2,
        compiler_params=LIMIT,
        cost_estimate=pl.CostEstimate(
            flops=10 * product.size, bytes_accessed=24 * product.size, transcendentals=1
        ),
    )(every, product, krylov)


def local(tokens, targets, gate_weight, up_weight, down_weight, krylov):
    rows, width = tokens.shape
    depth, span = gate_weight.shape
    own_rows = rows // (NY * NC)
    slab = width // NX
    at_x, at_z, at_y, at_c = (lax.axis_index(name) for name in ("x", "z", "y", "c"))

    gathered = lax.all_gather(
        jnp.concatenate([gate_weight, up_weight], 1), "z", axis=0, tiled=True
    )
    direction = krylov[KRYLOV - 1].astype(BF16)
    before, after = [direction], [direction]
    before.append(shift(direction, "z", 1))
    after.append(shift(direction, "z", -1))
    down_before, down_after = shift(down_weight, "x", 1), shift(down_weight, "x", -1)

    place = jnp.stack([at_x, at_y, at_c, at_z]).astype(jnp.int32)
    own, *sent = norm_tokens(place, tokens)
    before[1], after[1], down_before, down_after, own, sent = lax.optimization_barrier(
        (before[1], after[1], down_before, down_after, own, sent)
    )
    near = [shift(sent[ahead - 1], "x", ahead) for ahead in range(NX - 1, 0, -1)]
    before.append(shift(before[1], "z", 1))
    after.append(shift(after[1], "z", -1))
    middle = depth // 2
    down_far = [shift(down_before[:middle], "x", 1), shift(down_after[middle:], "x", -1)]
    before[2], after[2], near, down_far = lax.optimization_barrier(
        (before[2], after[2], near, down_far)
    )

    across = jnp.concatenate([down_weight, down_after, *down_far, down_before], 0)
    down_full = lax.all_gather(across, "z", axis=0, tiled=True)

    before.append(shift(before[2], "z", 1))
    after.append(shift(after[2], "z", -1))
    near = jnp.stack(near, 0)
    other = shift(near, "c", 1)
    far = [shift(before[3][:middle], "z", 1), shift(after[3][middle:], "z", -1)]
    parts = after + far + before[:0:-1]
    around, terms = forward_terms(place, own, near, other, gathered, parts)

    def arranged(values):
        values = rolled(values.reshape(own_rows, NX, NZ, depth), 1, at_x)
        return jnp.swapaxes(values, 1, 2).reshape(own_rows, width)

    start = (at_y * NC + at_c) * own_rows
    own_tokens, own_targets = (
        arranged(lax.dynamic_slice_in_dim(a, start, own_rows, 0)) for a in (tokens, targets)
    )
    turned = rolled(around.reshape(NX * rows, slab).T.reshape(NZ, depth, NX * rows), 0, at_z)
    gram = jnp.sum(krylov[:, None] * krylov[None], axis=(2, 3)).reshape(-1)
    forward = ring_sum([terms[d] for d in range(NX)], "x")
    gate, upward, tangent = jnp.split(forward, 3, axis=1)
    activated, derivative, curvature = gelu_parts(gate)
    hidden = (activated * upward).astype(BF16)
    hidden_tangent = (derivative * tangent * upward).astype(BF16)
    both = jnp.stack(
        [a.reshape(NC, NY, own_rows, span) for a in (hidden, hidden_tangent)], 1
    ).reshape(NC, 2 * NY * own_rows, span)
    both, down_full, turned, gram, own_tokens, own_targets = lax.optimization_barrier(
        (both, down_full, turned, gram, own_tokens, own_targets)
    )

    group = NY * own_rows
    theirs = contract(both[1], down_full, 1, 1).astype(BF16)
    theirs = [shift(theirs[kind * group : (kind + 1) * group], "c", 1) for kind in range(2)]
    mine = lax.optimization_barrier(contract(both[0], down_full, 1, 1).astype(BF16))
    mine = mine.reshape(2, NY, own_rows, width)
    sums = []
    for kind in range(2):
        arrived = theirs[kind].reshape(NY, own_rows, width)
        blocks = lax.optimization_barrier([added(mine[kind, d], arrived[d]) for d in range(NY)])
        sums.append(ring_sum(blocks, "y"))
    outputs, outputs_tangent = sums
    residual = (own_tokens.astype(F32) + outputs - own_targets.astype(F32)).astype(BF16)
    backs = []
    for values in (residual, outputs_tangent.astype(BF16)):
        chip = jnp.concatenate(ring_gather(values, "y"), 0)
        other = shift(chip, "c", 1)
        backs.append(
            jnp.concatenate(
                [jnp.dot(a, down_full, preferred_element_type=F32) for a in (chip, other)], 0
            )
        )
    backward, backward_tangent = backs
    gate_tangent = (
        (backward_tangent * derivative + backward * curvature * tangent) * upward
    ).astype(BF16)

    every = jnp.concatenate(ring_gather(gate_tangent, "x"), 0)
    blocks = [
        lax.optimization_barrier(contract(turned[d], every, 1, 0).astype(BF16))
        for d in range(NZ)
    ]
    product = ring_sum(blocks, "z") / (rows * NX * NZ)

    entries = width * span * NY * NC
    scaled = product / 4096.0
    sums = jnp.concatenate(
        [
            jnp.sum(krylov * product[None], axis=(1, 2)),
            gram,
            jnp.sum(scaled * scaled).reshape(1),
        ]
    )
    next_vector, row = finish(float(entries), exchanged(sums), product, krylov)
    return (next_vector, row[0, : KRYLOV + 1])


def solution(mesh):
    split = Mesh(mesh.devices.reshape(NX, NZ, NY, NC), ("x", "z", "y", "c"))
    dp, mp = ("x", "z"), ("y", "c")
    placed = (
        P(dp, None),
        P(dp, None),
        P(dp, mp),
        P(dp, mp),
        P(dp, mp),
        P(None, dp, mp),
    )
    return jax.shard_map(
        local, mesh=split, in_specs=placed, out_specs=(P(dp, mp), P()), check_vma=False
    )
```

```python
import math

import jax
import jax.numpy as jnp
from jax import lax
from jax.experimental import pallas as pl
from jax.experimental.pallas import tpu as pltpu
from jax.sharding import Mesh
from jax.sharding import PartitionSpec as P

KRYLOV = 4
NX, NZ, NY, NC = 4, 8, 4, 2

root_scale = math.sqrt(2.0 / math.pi)
cubic_term = 0.044715
epsilon = 1e-06

F32 = jnp.float32
BF16 = jnp.bfloat16


def gelu_parts(values):
    inside = root_scale * (values + cubic_term * values * values * values)
    hyperbolic = jnp.tanh(inside)
    rising = root_scale * (1.0 + 3.0 * cubic_term * values * values)
    falloff = 1.0 - hyperbolic * hyperbolic
    result = 0.5 * values * (1.0 + hyperbolic)
    derivative = 0.5 * (1.0 + hyperbolic) + 0.5 * values * falloff * rising
    curvature = falloff * rising + 0.5 * values * falloff * (
        6.0 * root_scale * cubic_term * values - 2.0 * hyperbolic * rising * rising
    )
    return (result, derivative, curvature)


def contract(left, right, left_dim, right_dim):
    return lax.dot_general(
        left, right, (((left_dim,), (right_dim,)), ((), ())), preferred_element_type=F32
    )


def shift(value, axis, by):
    size = lax.axis_size(axis)
    return lax.ppermute(value, axis, [(i, (i + by) % size) for i in range(size)])


def rolled(value, dim, start):
    size = value.shape[dim]
    return lax.dynamic_slice_in_dim(jnp.concatenate([value, value], dim), start, size, dim)


def added(first, second):
    return (first.astype(F32) + second.astype(F32)).astype(BF16)


def added_front(whole, front):
    return lax.dynamic_update_slice_in_dim(whole, added(whole[: front.shape[0]], front), 0, 0)


def added_back(whole, back):
    rows = whole.shape[0] - back.shape[0]
    return lax.dynamic_update_slice_in_dim(whole, added(whole[rows:], back), rows, 0)


def ring_sum(blocks, axis):
    size = len(blocks)
    far = size // 2
    half = blocks[far].shape[0] // 2
    ahead = shift(blocks[far][:half], axis, 1)
    behind = shift(blocks[far][half:], axis, -1)
    onward = added_front(blocks[far - 1], ahead)
    backward = added_back(blocks[far + 1], behind)
    for step in range(far - 1, 0, -1):
        ahead = shift(onward, axis, 1)
        behind = shift(backward, axis, -1)
        if step > 1:
            onward = added(blocks[step - 1], ahead)
            backward = added(blocks[size - step + 1], behind)
    return blocks[0].astype(F32) + ahead.astype(F32) + behind.astype(F32)


def direct_sum(blocks, axis):
    size = len(blocks)
    far = size // 2
    farthest = shift(blocks[far], axis, far)
    onward, backward = blocks[far - 1], blocks[far + 1]
    for step in range(far - 1, 0, -1):
        ahead = shift(onward, axis, 1)
        behind = shift(backward, axis, -1)
        if step > 1:
            onward = added(blocks[step - 1], ahead)
            backward = added(blocks[size - step + 1], behind)
    near = blocks[0].astype(F32) + ahead.astype(F32) + behind.astype(F32)
    return near + farthest.astype(F32)


def ring_gather(own, axis):
    far = lax.axis_size(axis) // 2
    half = own.shape[0] // 2
    before, after = [own], [own]
    for _ in range(1, far):
        before.append(shift(before[-1], axis, 1))
        after.append(shift(after[-1], axis, -1))
    farthest = jnp.concatenate(
        [shift(before[-1][:half], axis, 1), shift(after[-1][half:], axis, -1)], 0
    )
    return after + [farthest] + before[:0:-1]


def exchanged(value):
    devices = NX * NZ * NY * NC
    mine = jnp.zeros((128,), F32).at[: value.shape[0]].set(value)
    return lax.all_to_all(
        jnp.broadcast_to(mine, (devices, 128)), ("x", "z", "y", "c"), 0, 0, tiled=True
    )


VMEM = pl.BlockSpec(memory_space=pltpu.VMEM)
SMEM = pl.BlockSpec(memory_space=pltpu.SMEM)
LIMIT = pltpu.CompilerParams(vmem_limit_bytes=40 * 1024 * 1024)


def norm_kernel(place, tokens, own, *rest):
    sent, held = rest[: NX - 1], rest[NX - 1]
    count = held.shape[0]
    slab = own.shape[1]
    at_x, at_y, at_c = place[0], place[1], place[2]
    for c in range(NC):
        for y in range(NY):
            group = lax.rem(at_y + y, NY) * NC + lax.rem(at_c + c, NC)
            start = pl.multiple_of(group * count, count)
            values = tokens[pl.ds(start, count), :].astype(F32)
            square = jnp.mean(values * values, axis=1, keepdims=True)
            held[...] = (values * lax.rsqrt(square + epsilon)).astype(BF16)
            at = pl.ds((c * NY + y) * count, count)
            for ahead in range(NX if c == 0 else 1):
                columns = pl.ds(pl.multiple_of(lax.rem(at_x + ahead, NX) * slab, slab), slab)
                target = own if ahead == 0 else sent[ahead - 1]
                target[at, :] = held[:, columns]


def norm_tokens(place, tokens):
    rows, width = tokens.shape
    slab = width // NX
    shapes = [jax.ShapeDtypeStruct((rows, slab), BF16)]
    shapes += [jax.ShapeDtypeStruct((rows // NC, slab), BF16)] * (NX - 1)
    return pl.pallas_call(
        norm_kernel,
        out_shape=shapes,
        in_specs=[SMEM, VMEM],
        out_specs=[VMEM] * NX,
        scratch_shapes=[pltpu.VMEM((rows // (NC * NY), width), BF16)],
        compiler_params=LIMIT,
        cost_estimate=pl.CostEstimate(
            flops=4 * rows * width, bytes_accessed=4 * rows * width, transcendentals=rows
        ),
    )(place, tokens)


def forward_kernel(place, own, near, other, gathered, *rest):
    parts, (around, terms, matrix) = rest[: NZ + 1], rest[NZ + 1 :]
    depth = parts[0].shape[0]
    half = near.shape[1]
    two = gathered.shape[1]
    at = 0
    for part in parts:
        count = part.shape[0]
        ahead, offset = at // depth, at % depth
        start = lax.rem(place[3] + ahead, NZ) * depth + offset
        matrix[pl.ds(pl.multiple_of(start, count), count), :] = part[...]
        at += count
    around[0] = own[...]
    for d in range(1, NX):
        around[d, :half, :] = near[d - 1]
        around[d, half:, :] = other[d - 1]
    for d in range(NX):
        terms[d, :, :two] = jnp.dot(
            around[d], gathered[...], preferred_element_type=F32
        ).astype(BF16)
        terms[d, :, two:] = jnp.dot(
            around[d], matrix[...], preferred_element_type=F32
        ).astype(BF16)


def forward_terms(place, own, near, other, gathered, parts):
    rows, slab = own.shape
    span = parts[0].shape[1]
    width = gathered.shape[1] + span
    return pl.pallas_call(
        forward_kernel,
        out_shape=[
            jax.ShapeDtypeStruct((NX, rows, slab), BF16),
            jax.ShapeDtypeStruct((NX, rows, width), BF16),
        ],
        in_specs=[SMEM] + [VMEM] * (4 + len(parts)),
        out_specs=[VMEM] * 2,
        scratch_shapes=[pltpu.VMEM((slab, span), BF16)],
        compiler_params=LIMIT,
        cost_estimate=pl.CostEstimate(
            flops=2 * NX * rows * slab * width,
            bytes_accessed=2 * (2 * NX * rows * slab + slab * width + NX * rows * width),
            transcendentals=0,
        ),
    )(place, own, near, other, gathered, *parts)


def end_kernel(entries, every, product, krylov, vector, coefficients):
    sums = jnp.sum(every[...], axis=0, keepdims=True)
    lane = lax.broadcasted_iota(jnp.int32, sums.shape, 1)

    def at(place):
        return jnp.sum(jnp.where(lane == place, sums, 0.0), axis=1, keepdims=True)

    projections = [at(i) / entries for i in range(KRYLOV)]
    mean_square = at(KRYLOV + KRYLOV * KRYLOV) * (4096.0 * 4096.0 / entries)
    for i in range(KRYLOV):
        mean_square -= 2.0 * projections[i] * projections[i]
    for i in range(KRYLOV):
        for j in range(KRYLOV):
            gram = at(KRYLOV + KRYLOV * i + j) / entries
            mean_square += projections[i] * projections[j] * gram
    norm_value = jnp.sqrt(jnp.maximum(mean_square, 0.0) + epsilon)
    row = jnp.where(lane == KRYLOV, norm_value, 0.0)
    projected = product[...]
    for i in range(KRYLOV):
        projected -= projections[i] * krylov[i]
        row = jnp.where(lane == i, projections[i], row)
    vector[...] = projected / norm_value
    coefficients[...] = row


def finish(entries, every, product, krylov):
    return pl.pallas_call(
        lambda *refs: end_kernel(entries, *refs),
        out_shape=[
            jax.ShapeDtypeStruct(product.shape, F32),
            jax.ShapeDtypeStruct((1, every.shape[1]), F32),
        ],
        in_specs=[VMEM] * 3,
        out_specs=[VMEM] * 2,
        compiler_params=LIMIT,
        cost_estimate=pl.CostEstimate(
            flops=10 * product.size, bytes_accessed=24 * product.size, transcendentals=1
        ),
    )(every, product, krylov)


def local(tokens, targets, gate_weight, up_weight, down_weight, krylov):
    rows, width = tokens.shape
    depth, span = gate_weight.shape
    own_rows = rows // (NY * NC)
    slab = width // NX
    at_x, at_z, at_y, at_c = (lax.axis_index(name) for name in ("x", "z", "y", "c"))

    gathered = lax.all_gather(
        jnp.concatenate([gate_weight, up_weight], 1), "z", axis=0, tiled=True
    )
    direction = krylov[KRYLOV - 1].astype(BF16)
    before, after = [direction], [direction]
    before.append(shift(direction, "z", 1))
    after.append(shift(direction, "z", -1))
    down_before, down_after = shift(down_weight, "x", 1), shift(down_weight, "x", -1)

    place = jnp.stack([at_x, at_y, at_c, at_z]).astype(jnp.int32)
    own, *sent = norm_tokens(place, tokens)
    before[1], after[1], down_before, down_after, own, sent = lax.optimization_barrier(
        (before[1], after[1], down_before, down_after, own, sent)
    )
    near = [shift(sent[ahead - 1], "x", ahead) for ahead in range(NX - 1, 0, -1)]
    before.append(shift(before[1], "z", 1))
    after.append(shift(after[1], "z", -1))
    middle = depth // 2
    down_far = [shift(down_before[:middle], "x", 1), shift(down_after[middle:], "x", -1)]
    before[2], after[2], near, down_far = lax.optimization_barrier(
        (before[2], after[2], near, down_far)
    )

    across = jnp.concatenate([down_weight, down_after, *down_far, down_before], 0)
    down_full = lax.all_gather(across, "z", axis=0, tiled=True)

    before.append(shift(before[2], "z", 1))
    after.append(shift(after[2], "z", -1))
    near = jnp.stack(near, 0)
    other = shift(near, "c", 1)
    far = [shift(before[3][:middle], "z", 1), shift(after[3][middle:], "z", -1)]
    parts = after + far + before[:0:-1]
    around, terms = forward_terms(place, own, near, other, gathered, parts)

    def arranged(values):
        values = rolled(values.reshape(own_rows, NX, NZ, depth), 1, at_x)
        return jnp.swapaxes(values, 1, 2).reshape(own_rows, width)

    start = (at_y * NC + at_c) * own_rows
    own_tokens, own_targets = (
        arranged(lax.dynamic_slice_in_dim(a, start, own_rows, 0)) for a in (tokens, targets)
    )
    turned = rolled(around.reshape(NX * rows, slab).T.reshape(NZ, depth, NX * rows), 0, at_z)
    gram = jnp.sum(krylov[:, None] * krylov[None], axis=(2, 3)).reshape(-1)
    forward = ring_sum([terms[d] for d in range(NX)], "x")
    gate, upward, tangent = jnp.split(forward, 3, axis=1)
    activated, derivative, curvature = gelu_parts(gate)
    hidden = (activated * upward).astype(BF16)
    hidden_tangent = (derivative * tangent * upward).astype(BF16)
    both = jnp.stack(
        [a.reshape(NC, NY, own_rows, span) for a in (hidden, hidden_tangent)], 1
    ).reshape(NC, 2 * NY * own_rows, span)
    both, down_full, turned, gram, own_tokens, own_targets = lax.optimization_barrier(
        (both, down_full, turned, gram, own_tokens, own_targets)
    )

    group = NY * own_rows
    theirs = contract(both[1], down_full, 1, 1).astype(BF16)
    theirs = [shift(theirs[kind * group : (kind + 1) * group], "c", 1) for kind in range(2)]
    mine = lax.optimization_barrier(contract(both[0], down_full, 1, 1).astype(BF16))
    mine = mine.reshape(2, NY, own_rows, width)
    sums = []
    for kind in range(2):
        arrived = theirs[kind].reshape(NY, own_rows, width)
        blocks = lax.optimization_barrier([added(mine[kind, d], arrived[d]) for d in range(NY)])
        sums.append(ring_sum(blocks, "y"))
    outputs, outputs_tangent = sums
    residual = (own_tokens.astype(F32) + outputs - own_targets.astype(F32)).astype(BF16)
    backs = []
    for values in (residual, outputs_tangent.astype(BF16)):
        chip = jnp.concatenate(ring_gather(values, "y"), 0)
        other = shift(chip, "c", 1)
        backs.append(
            jnp.concatenate(
                [jnp.dot(a, down_full, preferred_element_type=F32) for a in (chip, other)], 0
            )
        )
    backward, backward_tangent = backs
    gate_tangent = (
        (backward_tangent * derivative + backward * curvature * tangent) * upward
    ).astype(BF16)

    every = jnp.concatenate(ring_gather(gate_tangent, "x"), 0)
    blocks = [
        lax.optimization_barrier(contract(turned[d], every, 1, 0).astype(BF16))
        for d in range(NZ)
    ]
    product = direct_sum(blocks, "z") / (rows * NX * NZ)

    entries = width * span * NY * NC
    scaled = product / 4096.0
    sums = jnp.concatenate(
        [
            jnp.sum(krylov * product[None], axis=(1, 2)),
            gram,
            jnp.sum(scaled * scaled).reshape(1),
        ]
    )
    next_vector, row = finish(float(entries), exchanged(sums), product, krylov)
    return (next_vector, row[0, : KRYLOV + 1])


def solution(mesh):
    split = Mesh(mesh.devices.reshape(NX, NZ, NY, NC), ("x", "z", "y", "c"))
    dp, mp = ("x", "z"), ("y", "c")
    placed = (
        P(dp, None),
        P(dp, None),
        P(dp, mp),
        P(dp, mp),
        P(dp, mp),
        P(None, dp, mp),
    )
    return jax.shard_map(
        local, mesh=split, in_specs=placed, out_specs=(P(dp, mp), P()), check_vma=False
    )
```

```python
import math

import jax
import jax.numpy as jnp
from jax import lax
from jax.experimental import pallas as pl
from jax.experimental.pallas import tpu as pltpu
from jax.sharding import Mesh
from jax.sharding import PartitionSpec as P

KRYLOV = 4
NX, NZ, NY, NC = 4, 8, 4, 2

root_scale = math.sqrt(2.0 / math.pi)
cubic_term = 0.044715
epsilon = 1e-06

F32 = jnp.float32
BF16 = jnp.bfloat16


def gelu_parts(values):
    inside = root_scale * (values + cubic_term * values * values * values)
    hyperbolic = jnp.tanh(inside)
    rising = root_scale * (1.0 + 3.0 * cubic_term * values * values)
    falloff = 1.0 - hyperbolic * hyperbolic
    result = 0.5 * values * (1.0 + hyperbolic)
    derivative = 0.5 * (1.0 + hyperbolic) + 0.5 * values * falloff * rising
    curvature = falloff * rising + 0.5 * values * falloff * (
        6.0 * root_scale * cubic_term * values - 2.0 * hyperbolic * rising * rising
    )
    return (result, derivative, curvature)


def contract(left, right, left_dim, right_dim):
    return lax.dot_general(
        left, right, (((left_dim,), (right_dim,)), ((), ())), preferred_element_type=F32
    )


def shift(value, axis, by):
    size = lax.axis_size(axis)
    return lax.ppermute(value, axis, [(i, (i + by) % size) for i in range(size)])


def rolled(value, dim, start):
    size = value.shape[dim]
    return lax.dynamic_slice_in_dim(jnp.concatenate([value, value], dim), start, size, dim)


def added(first, second):
    return (first.astype(F32) + second.astype(F32)).astype(BF16)


def added_front(whole, front):
    return lax.dynamic_update_slice_in_dim(whole, added(whole[: front.shape[0]], front), 0, 0)


def added_back(whole, back):
    rows = whole.shape[0] - back.shape[0]
    return lax.dynamic_update_slice_in_dim(whole, added(whole[rows:], back), rows, 0)


def ring_sum(blocks, axis):
    size = len(blocks)
    far = size // 2
    half = blocks[far].shape[0] // 2
    ahead = shift(blocks[far][:half], axis, 1)
    behind = shift(blocks[far][half:], axis, -1)
    onward = added_front(blocks[far - 1], ahead)
    backward = added_back(blocks[far + 1], behind)
    for step in range(far - 1, 0, -1):
        ahead = shift(onward, axis, 1)
        behind = shift(backward, axis, -1)
        if step > 1:
            onward = added(blocks[step - 1], ahead)
            backward = added(blocks[size - step + 1], behind)
    return blocks[0].astype(F32) + ahead.astype(F32) + behind.astype(F32)


def direct_sum(blocks, axis):
    size = len(blocks)
    far = size // 2
    farthest = shift(blocks[far], axis, far)
    onward, backward = blocks[far - 1], blocks[far + 1]
    for step in range(far - 1, 0, -1):
        ahead = shift(onward, axis, 1)
        behind = shift(backward, axis, -1)
        if step > 1:
            onward = added(blocks[step - 1], ahead)
            backward = added(blocks[size - step + 1], behind)
    near = blocks[0].astype(F32) + ahead.astype(F32) + behind.astype(F32)
    return near + farthest.astype(F32)


def ring_gather(own, axis):
    far = lax.axis_size(axis) // 2
    half = own.shape[0] // 2
    before, after = [own], [own]
    for _ in range(1, far):
        before.append(shift(before[-1], axis, 1))
        after.append(shift(after[-1], axis, -1))
    farthest = jnp.concatenate(
        [shift(before[-1][:half], axis, 1), shift(after[-1][half:], axis, -1)], 0
    )
    return after + [farthest] + before[:0:-1]


def exchanged(value):
    devices = NX * NZ * NY * NC
    mine = jnp.zeros((128,), F32).at[: value.shape[0]].set(value)
    return lax.all_to_all(
        jnp.broadcast_to(mine, (devices, 128)), ("x", "z", "y", "c"), 0, 0, tiled=True
    )


VMEM = pl.BlockSpec(memory_space=pltpu.VMEM)
SMEM = pl.BlockSpec(memory_space=pltpu.SMEM)
LIMIT = pltpu.CompilerParams(vmem_limit_bytes=40 * 1024 * 1024)


def norm_kernel(place, tokens, own, *rest):
    sent, held = rest[: NX - 1], rest[NX - 1]
    count = held.shape[0]
    slab = own.shape[1]
    at_x, at_y, at_c = place[0], place[1], place[2]
    for c in range(NC):
        for y in range(NY):
            group = lax.rem(at_y + y, NY) * NC + lax.rem(at_c + c, NC)
            start = pl.multiple_of(group * count, count)
            values = tokens[pl.ds(start, count), :].astype(F32)
            square = jnp.mean(values * values, axis=1, keepdims=True)
            held[...] = (values * lax.rsqrt(square + epsilon)).astype(BF16)
            at = pl.ds((c * NY + y) * count, count)
            for ahead in range(NX if c == 0 else 1):
                columns = pl.ds(pl.multiple_of(lax.rem(at_x + ahead, NX) * slab, slab), slab)
                target = own if ahead == 0 else sent[ahead - 1]
                target[at, :] = held[:, columns]


def norm_tokens(place, tokens):
    rows, width = tokens.shape
    slab = width // NX
    shapes = [jax.ShapeDtypeStruct((rows, slab), BF16)]
    shapes += [jax.ShapeDtypeStruct((rows // NC, slab), BF16)] * (NX - 1)
    return pl.pallas_call(
        norm_kernel,
        out_shape=shapes,
        in_specs=[SMEM, VMEM],
        out_specs=[VMEM] * NX,
        scratch_shapes=[pltpu.VMEM((rows // (NC * NY), width), BF16)],
        compiler_params=LIMIT,
        cost_estimate=pl.CostEstimate(
            flops=4 * rows * width, bytes_accessed=4 * rows * width, transcendentals=rows
        ),
    )(place, tokens)


def forward_kernel(place, own, near, other, gathered, *rest):
    parts, (around, terms, matrix) = rest[: NZ + 1], rest[NZ + 1 :]
    depth = parts[0].shape[0]
    half = near.shape[1]
    two = gathered.shape[1]
    at = 0
    for part in parts:
        count = part.shape[0]
        ahead, offset = at // depth, at % depth
        start = lax.rem(place[3] + ahead, NZ) * depth + offset
        matrix[pl.ds(pl.multiple_of(start, count), count), :] = part[...]
        at += count
    around[0] = own[...]
    for d in range(1, NX):
        around[d, :half, :] = near[d - 1]
        around[d, half:, :] = other[d - 1]
    for d in range(NX):
        terms[d, :, :two] = jnp.dot(
            around[d], gathered[...], preferred_element_type=F32
        ).astype(BF16)
        terms[d, :, two:] = jnp.dot(
            around[d], matrix[...], preferred_element_type=F32
        ).astype(BF16)


def forward_terms(place, own, near, other, gathered, parts):
    rows, slab = own.shape
    span = parts[0].shape[1]
    width = gathered.shape[1] + span
    return pl.pallas_call(
        forward_kernel,
        out_shape=[
            jax.ShapeDtypeStruct((NX, rows, slab), BF16),
            jax.ShapeDtypeStruct((NX, rows, width), BF16),
        ],
        in_specs=[SMEM] + [VMEM] * (4 + len(parts)),
        out_specs=[VMEM] * 2,
        scratch_shapes=[pltpu.VMEM((slab, span), BF16)],
        compiler_params=LIMIT,
        cost_estimate=pl.CostEstimate(
            flops=2 * NX * rows * slab * width,
            bytes_accessed=2 * (2 * NX * rows * slab + slab * width + NX * rows * width),
            transcendentals=0,
        ),
    )(place, own, near, other, gathered, *parts)


def end_kernel(entries, every, product, krylov, vector, coefficients):
    sums = jnp.sum(every[...], axis=0, keepdims=True)
    lane = lax.broadcasted_iota(jnp.int32, sums.shape, 1)

    def at(place):
        return jnp.sum(jnp.where(lane == place, sums, 0.0), axis=1, keepdims=True)

    projections = [at(i) / entries for i in range(KRYLOV)]
    mean_square = at(KRYLOV + KRYLOV * KRYLOV) * (4096.0 * 4096.0 / entries)
    for i in range(KRYLOV):
        mean_square -= 2.0 * projections[i] * projections[i]
    for i in range(KRYLOV):
        for j in range(KRYLOV):
            gram = at(KRYLOV + KRYLOV * i + j) / entries
            mean_square += projections[i] * projections[j] * gram
    norm_value = jnp.sqrt(jnp.maximum(mean_square, 0.0) + epsilon)
    row = jnp.where(lane == KRYLOV, norm_value, 0.0)
    projected = product[...]
    for i in range(KRYLOV):
        projected -= projections[i] * krylov[i]
        row = jnp.where(lane == i, projections[i], row)
    vector[...] = projected / norm_value
    coefficients[...] = row


def finish(entries, every, product, krylov):
    return pl.pallas_call(
        lambda *refs: end_kernel(entries, *refs),
        out_shape=[
            jax.ShapeDtypeStruct(product.shape, F32),
            jax.ShapeDtypeStruct((1, every.shape[1]), F32),
        ],
        in_specs=[VMEM] * 3,
        out_specs=[VMEM] * 2,
        compiler_params=LIMIT,
        cost_estimate=pl.CostEstimate(
            flops=10 * product.size, bytes_accessed=24 * product.size, transcendentals=1
        ),
    )(every, product, krylov)


def local(tokens, targets, gate_weight, up_weight, down_weight, krylov):
    rows, width = tokens.shape
    depth, span = gate_weight.shape
    own_rows = rows // (NY * NC)
    slab = width // NX
    at_x, at_z, at_y, at_c = (lax.axis_index(name) for name in ("x", "z", "y", "c"))

    gathered = lax.all_gather(
        jnp.concatenate([gate_weight, up_weight], 1), "z", axis=0, tiled=True
    )
    direction = krylov[KRYLOV - 1].astype(BF16)
    before, after = [direction], [direction]
    before.append(shift(direction, "z", 1))
    after.append(shift(direction, "z", -1))
    down_before, down_after = shift(down_weight, "x", 1), shift(down_weight, "x", -1)

    place = jnp.stack([at_x, at_y, at_c, at_z]).astype(jnp.int32)
    own, *sent = norm_tokens(place, tokens)
    before[1], after[1], down_before, down_after, own, sent = lax.optimization_barrier(
        (before[1], after[1], down_before, down_after, own, sent)
    )
    near = [shift(sent[ahead - 1], "x", ahead) for ahead in range(NX - 1, 0, -1)]
    before.append(shift(before[1], "z", 1))
    after.append(shift(after[1], "z", -1))
    middle = depth // 2
    down_far = [shift(down_before[:middle], "x", 1), shift(down_after[middle:], "x", -1)]
    before[2], after[2], near, down_far = lax.optimization_barrier(
        (before[2], after[2], near, down_far)
    )

    across = jnp.concatenate([down_weight, down_after, *down_far, down_before], 0)
    down_full = lax.all_gather(across, "z", axis=0, tiled=True)

    before.append(shift(before[2], "z", 1))
    after.append(shift(after[2], "z", -1))
    near = jnp.stack(near, 0)
    other = shift(near, "c", 1)
    far = [shift(before[3][:middle], "z", 1), shift(after[3][middle:], "z", -1)]
    parts = after + far + before[:0:-1]
    around, terms = forward_terms(place, own, near, other, gathered, parts)

    def arranged(values):
        values = rolled(values.reshape(own_rows, NX, NZ, depth), 1, at_x)
        return jnp.swapaxes(values, 1, 2).reshape(own_rows, width)

    start = (at_y * NC + at_c) * own_rows
    own_tokens, own_targets = (
        arranged(lax.dynamic_slice_in_dim(a, start, own_rows, 0)) for a in (tokens, targets)
    )
    turned = rolled(around.reshape(NX * rows, slab).T.reshape(NZ, depth, NX * rows), 0, at_z)
    gram = jnp.sum(krylov[:, None] * krylov[None], axis=(2, 3)).reshape(-1)
    forward = ring_sum([terms[d] for d in range(NX)], "x")
    gate, upward, tangent = jnp.split(forward, 3, axis=1)
    activated, derivative, curvature = gelu_parts(gate)
    hidden = (activated * upward).astype(BF16)
    hidden_tangent = (derivative * tangent * upward).astype(BF16)
    both = jnp.stack(
        [a.reshape(NC, NY, own_rows, span) for a in (hidden, hidden_tangent)], 1
    ).reshape(NC, 2 * NY * own_rows, span)
    both, down_full, turned, gram, own_tokens, own_targets = lax.optimization_barrier(
        (both, down_full, turned, gram, own_tokens, own_targets)
    )

    group = NY * own_rows
    theirs = contract(both[1], down_full, 1, 1).astype(BF16)
    theirs = [shift(theirs[kind * group : (kind + 1) * group], "c", 1) for kind in range(2)]
    mine = lax.optimization_barrier(contract(both[0], down_full, 1, 1).astype(BF16))
    mine = mine.reshape(2, NY, own_rows, width)
    sums = []
    for kind in range(2):
        arrived = theirs[kind].reshape(NY, own_rows, width)
        blocks = lax.optimization_barrier([added(mine[kind, d], arrived[d]) for d in range(NY)])
        sums.append(ring_sum(blocks, "y"))
    outputs, outputs_tangent = sums
    residual = (own_tokens.astype(F32) + outputs - own_targets.astype(F32)).astype(BF16)
    backs = []
    for values in (residual, outputs_tangent.astype(BF16)):
        chip = jnp.concatenate(ring_gather(values, "y"), 0)
        other = shift(chip, "c", 1)
        backs.append(
            jnp.concatenate(
                [jnp.dot(a, down_full, preferred_element_type=F32) for a in (chip, other)], 0
            )
        )
    backward, backward_tangent = backs
    gate_tangent = (
        (backward_tangent * derivative + backward * curvature * tangent) * upward
    ).astype(BF16)

    cut = rows // NC
    rings = [ring_gather(part, "x") for part in (gate_tangent[:cut], gate_tangent[cut:])]
    every = jnp.concatenate([ring[d] for d in range(NX) for ring in rings], 0)
    blocks = [
        lax.optimization_barrier(contract(turned[d], every, 1, 0).astype(BF16))
        for d in range(NZ)
    ]
    product = direct_sum(blocks, "z") / (rows * NX * NZ)

    entries = width * span * NY * NC
    scaled = product / 4096.0
    sums = jnp.concatenate(
        [
            jnp.sum(krylov * product[None], axis=(1, 2)),
            gram,
            jnp.sum(scaled * scaled).reshape(1),
        ]
    )
    next_vector, row = finish(float(entries), exchanged(sums), product, krylov)
    return (next_vector, row[0, : KRYLOV + 1])


def solution(mesh):
    split = Mesh(mesh.devices.reshape(NX, NZ, NY, NC), ("x", "z", "y", "c"))
    dp, mp = ("x", "z"), ("y", "c")
    placed = (
        P(dp, None),
        P(dp, None),
        P(dp, mp),
        P(dp, mp),
        P(dp, mp),
        P(None, dp, mp),
    )
    return jax.shard_map(
        local, mesh=split, in_specs=placed, out_specs=(P(dp, mp), P()), check_vma=False
    )
```
